512 devices in a mesh: smp: 128 (over x_lo, z, y), par: 4 (over x_hi, core).
Axes of the slice: x: 4 (x_hi: 2, x_lo: 2; x = x_hi * 2 + x_lo), y: 4, z: 16, core: 2. Of those that a mesh axis runs over, the one named last changes fastest.
Arguments:
- derivatives: bfloat16 [10240, 2048], P('smp', 'par'), may hold values from -40 to 40
- epsilon: float32 [10240], P('smp'), may hold values from -6 to 6
Outputs:
- gram_tile: float32 [10240, 10240], P('smp', 'par')
- update: float32 [2048], P('par')
The draws below stay inside these ranges and needn't reach their ends.
All inputs are finite; a program needn't handle non-finite values.
Results may differ from the reference program's by a relative error of at most 0.003.
Values may be sent and summed in bfloat16 or wider, within the bound.
A program may use at most 64 MiB of HBM per device.

```python
import math
import jax
import jax.numpy as jnp
from jax import lax

P_SIZE = 2048
SAMPLES = 10240


def draw_derivatives(key, part):
    keys = jax.random.split(key, 3)
    noise = jnp.clip(jax.random.normal(keys[0], (SAMPLES, P_SIZE), jnp.float32), -6.0, 6.0)
    row_scale = jnp.exp(jax.random.uniform(keys[1], (SAMPLES, 1), jnp.float32, math.log(0.5), math.log(5.0)))
    column_base = jax.random.uniform(keys[2], (1, P_SIZE), jnp.float32, -1.5, 1.5)
    ramp = 1.0 + 2.0 * jnp.arange(SAMPLES, dtype=jnp.float32)[:, None] / SAMPLES
    values = noise * row_scale + column_base * ramp
    return values.astype(jnp.bfloat16)


def levels(own_key, dims, pieces, least, largest):
    level, own = 1.0, jax.random.fold_in(own_key, 6)
    for axis_at, shards_of in pieces:
        steps = jnp.exp(jax.random.uniform(jax.random.fold_in(own, axis_at), (shards_of,), jnp.float32, least / len(pieces), largest / len(pieces)))
        level = level * jnp.repeat(steps, dims[axis_at] // shards_of).reshape([-1 if axis == axis_at else 1 for axis in range(len(dims))])
    return level


def normal_values(key, shape, scale, most, cuts=(), held_as=jnp.bfloat16):
    values = jax.random.normal(key, shape, jnp.float32) * scale
    if len(cuts) > 0:
        values = levels(key, shape, cuts, -0.22, 0.18) * values
    return jnp.clip(values, min=-most, max=most).astype(held_as)


def setup_inputs(seed: int = 0) -> dict:
    key_of = jax.random.split(jax.random.key(seed), 3)
    derivatives = draw_derivatives(jax.random.fold_in(key_of[2], 71), 0)
    epsilon = normal_values(key_of[1], (SAMPLES,), 1.0, 6.0, ((0, 128),), jnp.float32)
    return {"derivatives": derivatives, "epsilon": epsilon}


def reference(derivatives, epsilon):
    widened = derivatives.astype(jnp.float32)
    column_mean = lax.optimization_barrier(jnp.sum(widened, axis=0)) / SAMPLES
    factor = 1.0 / math.sqrt(SAMPLES)
    centered = ((widened - column_mean) * factor).astype(jnp.bfloat16)
    gram_tile = jnp.dot(centered, centered.T, preferred_element_type=jnp.float32)
    update = jnp.dot(epsilon, centered.astype(jnp.float32), precision=lax.Precision.HIGHEST)
    return (gram_tile, update)
```

```python
import functools
import math

import jax
import jax.numpy as jnp
from jax import lax
from jax.experimental import pallas as pl
from jax.experimental.pallas import tpu as pltpu
from jax.sharding import PartitionSpec as P

MESH = pl.DeviceIdType.MESH
F32, BF16 = jnp.float32, jnp.bfloat16
ROWS, COLS = 80, 512
NZ, NY = 16, 4
SUB = 2
WIDTH = COLS // SUB
PIECES = 2 * SUB
STAT = 2 * COLS + 128
PARENT = {1: 0, 2: 1, 3: 2, 4: 0, 5: 4, 6: 5, 7: 6, 8: 7}
ORDER = (1, 4, 2, 5, 3, 6, 7, 8)


def children(s, most):
    return [q for q in range(1, most + 1) if PARENT[q] == s]


def device(xh, xl, y, z, c):
    return (xl * 64 + z * NY + y, xh * 2 + c)


def kernel(total, d_ref, eps_ref, gram_ref, upd_ref,
           q_raw, r_raw, q_c, r_c, z_stat, p_stat, mean, p_out, p_in,
           q_send, q_recv, r_src, r_send, r_recv, zs_send, zs_recv, ps_send, ps_recv, o_send, o_recv):
    s_at, p_at = lax.axis_index("smp"), lax.axis_index("par")
    xl, z, y = s_at // 64, (s_at // NY) % NZ, s_at % NY
    xh, c = p_at // 2, p_at % 2
    other = 1 - c
    half, z_lo = z // 8, z % 8
    me = xl * NY + y
    factor = 1.0 / math.sqrt(total)

    def at_z(step):
        return (z + step + NZ) % NZ

    barrier = pltpu.get_barrier_semaphore()

    def greet(where):
        pl.semaphore_signal(barrier, inc=1, device_id=where, device_id_type=MESH)

    for k in range(1, NZ):
        greet(device(xh, xl, y, at_z(k), c))
    near = [k for k in (1, -1, 4, -4)]
    for k in near:
        greet(device(xh, xl, y, at_z(k), other))
    greet(device(xh, xl, y, z, other))
    for k in range(1, 8):
        g = (me + k) % 8
        for cc in range(2):
            greet(device(xh, g // NY, g % NY, z, cc))
    same = (xl == xh)
    for k in range(8):
        src_xh, src_y = k // NY, k % NY
        is_me = same & (src_xh == xh) & (src_y == y)

        @pl.when(jnp.logical_not(is_me))
        def _():
            greet(device(src_xh, xh, src_y, z, c))

    d = d_ref[...].astype(F32)
    eps = eps_ref[...]
    sums = jnp.sum(d, axis=0, keepdims=True)
    weighted = lax.dot_general(eps, d, (((1,), (0,)), ((), ())), precision=lax.Precision.HIGHEST,
                               preferred_element_type=F32)
    z_stat[z, :, 0:COLS] = sums
    z_stat[z, :, COLS:2 * COLS] = weighted
    z_stat[z, :, 2 * COLS:] = jnp.broadcast_to(jnp.sum(eps, axis=1, keepdims=True), (1, 128))

    pl.semaphore_wait(barrier, 15 + len(near) + 1 + 14 + 8 - same.astype(jnp.int32))

    started = []

    def send(src, dst, s_sem, r_sem, where):
        copy = pltpu.make_async_remote_copy(src_ref=src, dst_ref=dst, send_sem=s_sem, recv_sem=r_sem,
                                            device_id=where, device_id_type=MESH)
        copy.start()
        return copy

    def arrived(ref, sem):
        pltpu.make_async_remote_copy(src_ref=ref, dst_ref=ref, send_sem=sem, recv_sem=sem,
                                     device_id=(s_at, p_at), device_id_type=MESH).wait_recv()

    for k in range(1, NZ):
        started.append(send(z_stat.at[z], z_stat.at[z], zs_send.at[k], zs_recv.at[z],
                            device(xh, xl, y, at_z(k), c)))

    steps = [q for q in (4, 1)]
    targets = [q for q in steps] + [-q for q in steps]
    for i in range(SUB):
        for n, q in enumerate(targets):
            started.append(send(d_ref.at[:, pl.ds(i * WIDTH, WIDTH)], r_raw.at[z_lo, c * SUB + i],
                                r_src.at[n, i], r_recv.at[z_lo, c * SUB + i],
                                device(xh, xl, y, at_z(q), half)))

    def own_copy(i):
        return pltpu.make_async_copy(d_ref.at[:, pl.ds(i * WIDTH, WIDTH)], r_raw.at[z_lo, c * SUB + i],
                                     r_recv.at[z_lo, c * SUB + i])

    def own_send(i):
        return pltpu.make_async_remote_copy(
            src_ref=d_ref.at[:, pl.ds(i * WIDTH, WIDTH)], dst_ref=r_raw.at[z_lo, c * SUB + i],
            send_sem=r_src.at[4, i], recv_sem=r_recv.at[z_lo, c * SUB + i],
            device_id=device(xh, xl, y, z, other), device_id_type=MESH)

    for i in range(SUB):
        @pl.when(half == c)
        def _():
            own_copy(i).start()

        @pl.when(half != c)
        def _():
            own_send(i).start()

    for k in range(1, 8):
        g = (me + k) % 8
        started.append(send(d_ref, q_raw.at[me, c], q_send.at[k], q_recv.at[me, c],
                            device(xh, g // NY, g % NY, z, c)))
    started.append(send(d_ref, q_raw.at[me, c], q_send.at[0], q_recv.at[me, c], device(xh, xl, y, z, other)))

    def pass_on(sign, s, most):
        origin = at_z(-sign * s)

        @pl.when(origin // 8 == c)
        def _():
            lo = origin % 8
            for j in range(PIECES):
                arrived(r_raw.at[lo, j], r_recv.at[lo, j])
                for q in children(s, most):
                    send(r_raw.at[lo, j], r_raw.at[lo, j], r_send.at[lo, j], r_recv.at[lo, j],
                         device(xh, xl, y, at_z(sign * (q - s)), c))

    def pass_both(s):
        pass_on(1, s, 8)
        if s <= 7:
            pass_on(-1, s, 7)

    def forward_plane(k):
        g = (me + k) % 8
        arrived(q_raw.at[g, c], q_recv.at[g, c])
        started.append(send(q_raw.at[g, c], q_raw.at[g, c], q_send.at[8 + k], q_recv.at[g, c],
                            device(xh, xl, y, z, other)))

    pass_both(1)
    pass_both(4)
    pass_both(2)
    pass_both(5)

    for k in range(1, NZ):
        o = at_z(k)
        arrived(z_stat.at[o], zs_recv.at[o])
    total_z = z_stat[0]
    for k in range(1, NZ):
        total_z = total_z + z_stat[k]
    p_stat[me, c] = total_z
    for k in range(1, 8):
        g = (me + k) % 8
        for cc in range(2):
            started.append(send(p_stat.at[me, c], p_stat.at[me, c], ps_send.at[k, cc], ps_recv.at[me, c],
                                device(xh, g // NY, g % NY, z, (c + cc) % 2)))
    started.append(send(p_stat.at[me, c], p_stat.at[me, c], ps_send.at[0, 0], ps_recv.at[me, c],
                        device(xh, xl, y, z, other)))
    pass_both(3)
    for k in range(1, 8):
        forward_plane(k)
    pass_both(6)
    for k in range(8):
        g = (me + k) % 8
        for cc in range(2):
            o = (c + cc) % 2
            if k or cc:
                arrived(p_stat.at[g, o], ps_recv.at[g, o])
    wholes = []
    for o in range(2):
        whole = p_stat[0, o]
        for g in range(1, 8):
            whole = whole + p_stat[g, o]
        wholes.append(whole)
        mean[:, o * COLS:(o + 1) * COLS] = whole[:, 0:COLS] / total
    mine = jnp.where(c == 0, wholes[0], wholes[1])
    upd_ref[...] = (mine[:, COLS:2 * COLS] - (mine[:, 0:COLS] / total) * mine[:, 2 * COLS:2 * COLS + 1]) * factor

    def center(raw, columns):
        return ((raw.astype(F32) - mean[:, columns]) * factor).astype(BF16)

    q_c[pl.ds(me * ROWS, ROWS), pl.ds(pl.multiple_of(c * COLS, COLS), COLS)] = (
        (d_ref[...].astype(F32) - mean[:, pl.ds(pl.multiple_of(c * COLS, COLS), COLS)]) * factor).astype(BF16)
    arrived(q_raw.at[me, other], q_recv.at[me, other])
    q_c[pl.ds(me * ROWS, ROWS), pl.ds(pl.multiple_of(other * COLS, COLS), COLS)] = (
        (q_raw[me, other].astype(F32) - mean[:, pl.ds(pl.multiple_of(other * COLS, COLS), COLS)]) * factor
    ).astype(BF16)
    for k in range(1, 8):
        g = (me + k) % 8
        arrived(q_raw.at[g, other], q_recv.at[g, other])
        for o in range(2):
            q_c[pl.ds(g * ROWS, ROWS), o * COLS:(o + 1) * COLS] = center(q_raw[g, o], slice(o * COLS, (o + 1) * COLS))
    pass_both(7)
    pass_both(8)

    @pl.when(half == c)
    def _():
        for j in range(PIECES):
            arrived(r_raw.at[z_lo, j], r_recv.at[z_lo, j])

    for lo in range(8):
        for j in range(PIECES):
            r_c[lo * ROWS:(lo + 1) * ROWS, j * WIDTH:(j + 1) * WIDTH] = center(
                r_raw[lo, j], slice(j * WIDTH, (j + 1) * WIDTH))

    slot = xh * NY + y

    def product(t):
        part = lax.dot_general(q_c[t * 160:(t + 1) * 160, :], r_c[...], (((1,), (1,)), ((), ())),
                               preferred_element_type=F32).astype(BF16)
        for u in range(2):
            g = 2 * t + u
            p_out[g] = part[u * ROWS:(u + 1) * ROWS]
            is_me = same & (g == me)

            @pl.when(is_me)
            def _():
                pltpu.make_async_copy(p_out.at[g], p_in.at[slot], o_recv.at[slot]).start()

            @pl.when(jnp.logical_not(is_me))
            def _():
                send(p_out.at[g], p_in.at[slot], o_send.at[g], o_recv.at[slot],
                     device(xl, g // NY, g % NY, z, c))

    for t in range(4):
        product(t)

    for k in range(8):
        arrived(p_in.at[k], o_recv.at[k])

    for u in range(5):
        rows = slice(u * 16, (u + 1) * 16)
        added = [p_in[k, rows].astype(F32) + p_in[NY + k, rows].astype(F32) for k in range(NY)]
        for t in range(4):
            gram_ref[rows, t * 640:(t + 1) * 640] = jnp.concatenate(
                [added[k][:, (2 * t + v) * ROWS:(2 * t + v + 1) * ROWS] for v in range(2) for k in range(NY)], axis=1)

    for copy in started:
        copy.wait_send()
    for i in range(SUB):
        @pl.when(half != c)
        def _():
            own_send(i).wait_send()
    for sign, most in ((1, 8), (-1, 7)):
        for s in range(1, most):
            origin = at_z(-sign * s)
            if children(s, most):
                @pl.when(origin // 8 == c)
                def _():
                    lo = origin % 8
                    for j in range(PIECES):
                        pltpu.make_async_remote_copy(
                            src_ref=r_raw.at[lo, j], dst_ref=r_raw.at[lo, j], send_sem=r_send.at[lo, j],
                            recv_sem=r_recv.at[lo, j], device_id=(s_at, p_at), device_id_type=MESH).wait_send()
    for g in range(8):
        @pl.when(jnp.logical_not(same & (g == me)))
        def _():
            pltpu.make_async_remote_copy(
                src_ref=p_out.at[g], dst_ref=p_in.at[slot], send_sem=o_send.at[g], recv_sem=o_recv.at[slot],
                device_id=(s_at, p_at), device_id_type=MESH).wait_send()


def shards(derivatives, epsilon):
    total = derivatives.shape[0] * 128
    dma = pltpu.SemaphoreType.DMA
    gram, upd = pl.pallas_call(
        functools.partial(kernel, total),
        name="gram",
        out_shape=(jax.ShapeDtypeStruct((ROWS, 2560), F32), jax.ShapeDtypeStruct((1, COLS), F32)),
        in_specs=[pl.BlockSpec(memory_space=pltpu.VMEM)] * 2,
        out_specs=[pl.BlockSpec(memory_space=pltpu.VMEM)] * 2,
        scratch_shapes=[
            pltpu.VMEM((8, 2, ROWS, COLS), BF16),
            pltpu.VMEM((8, PIECES, ROWS, WIDTH), BF16),
            pltpu.VMEM((640, 2 * COLS), BF16),
            pltpu.VMEM((640, 2 * COLS), BF16),
            pltpu.VMEM((NZ, 1, STAT), F32),
            pltpu.VMEM((8, 2, 1, STAT), F32),
            pltpu.VMEM((1, 2 * COLS), F32),
            pltpu.VMEM((8, ROWS, 640), BF16),
            pltpu.VMEM((8, ROWS, 640), BF16),
            dma((16,)), dma((8, 2)),
            dma((5, SUB)), dma((8, PIECES)), dma((8, PIECES)),
            dma((NZ,)), dma((NZ,)),
            dma((8, 2)), dma((8, 2)),
            dma((8,)), dma((8,)),
        ],
        compiler_params=pltpu.CompilerParams(collective_id=0, has_side_effects=True, vmem_limit_bytes=48 << 20),
    )(derivatives, epsilon.reshape(1, ROWS))
    return gram, upd.reshape(COLS)


def solution(mesh):
    in_specs = (P("smp", "par"), P("smp"))
    out_specs = (P("smp", "par"), P("par"))
    return jax.shard_map(shards, mesh=mesh, in_specs=in_specs, out_specs=out_specs, check_vma=False)
```

```python
import functools
import math

import jax
import jax.numpy as jnp
from jax import lax
from jax.experimental import pallas as pl
from jax.experimental.pallas import tpu as pltpu
from jax.sharding import PartitionSpec as P

MESH = pl.DeviceIdType.MESH
F32, BF16 = jnp.float32, jnp.bfloat16
ROWS, COLS = 80, 512
NZ, NY = 16, 4
SUB = 2
WIDTH = COLS // SUB
PIECES = 2 * SUB
GROUP = 4 * ROWS
STAT = 2 * COLS + 128
NEAR = (1, -1, 2, -2, 3, -3)
FAR = 6
LOOP_FROM = 5


def device(xh, xl, y, z, c):
    return (xl * 64 + z * NY + y, xh * 2 + c)


def kernel(total, d_hbm, eps_ref, gram_ref, upd_ref,
           d_ref, q_raw, r_raw, q_c, r_c, stat, z_near, z_out, z_far, p_stat, mean, p_out, p_in,
           d_sem, q_send, q_recv, r_src, r_send, r_recv, zn_send, zn_recv, zf_send, zf_recv,
           ps_send, ps_recv, o_send, o_recv):
    s_at, p_at = lax.axis_index("smp"), lax.axis_index("par")
    xl, z, y = s_at // 64, (s_at // NY) % NZ, s_at % NY
    xh, c = p_at // 2, p_at % 2
    other = 1 - c
    half, z_lo = z // 8, z % 8
    me = xl * NY + y
    factor = 1.0 / math.sqrt(total)
    load = pltpu.make_async_copy(d_hbm, d_ref, d_sem)
    load.start()

    def at_z(step):
        return (z + step + NZ) % NZ

    barrier = pltpu.get_barrier_semaphore()

    def greet(where):
        pl.semaphore_signal(barrier, inc=1, device_id=where, device_id_type=MESH)

    same = (xl == xh)
    for k in range(8):
        src_xh, src_y = k // NY, k % NY

        @pl.when(jnp.logical_not(same & (src_xh == xh) & (src_y == y)))
        def _():
            greet(device(src_xh, xh, src_y, z, c))

    for k in NEAR:
        greet(device(xh, xl, y, at_z(k), c))
    for k in (1, -1):
        greet(device(xh, xl, y, at_z(k), other))
    for k in range(1, 8):
        g = (me + k) % 8
        for cc in range(2):
            greet(device(xh, g // NY, g % NY, z, cc))
    greet(device(xh, xl, y, z, other))

    load.wait()
    d = d_ref[...].astype(F32)
    eps = eps_ref[...]
    stat[:, 0:COLS] = jnp.sum(d, axis=0, keepdims=True)
    stat[:, COLS:2 * COLS] = lax.dot_general(
        eps, d, (((1,), (0,)), ((), ())), precision=lax.Precision.HIGHEST, preferred_element_type=F32)
    stat[:, 2 * COLS:] = jnp.broadcast_to(jnp.sum(eps, axis=1, keepdims=True), (1, 128))

    pl.semaphore_wait(barrier, 8 - same.astype(jnp.int32) + len(NEAR) + 2 + 14 + 1)

    started = []

    def send(src, dst, s_sem, r_sem, where):
        copy = pltpu.make_async_remote_copy(src_ref=src, dst_ref=dst, send_sem=s_sem, recv_sem=r_sem,
                                            device_id=where, device_id_type=MESH)
        copy.start()
        return copy

    def handle(ref, sem):
        return pltpu.make_async_remote_copy(src_ref=ref, dst_ref=ref, send_sem=sem, recv_sem=sem,
                                            device_id=(s_at, p_at), device_id_type=MESH)

    def arrived(ref, sem):
        handle(ref, sem).wait_recv()

    for n, k in enumerate(NEAR):
        started.append(send(stat, z_near.at[n], zn_send.at[n], zn_recv.at[n], device(xh, xl, y, at_z(-k), c)))

    for i in range(SUB):
        for n, q in enumerate((1, -1)):
            started.append(send(d_ref.at[:, pl.ds(i * WIDTH, WIDTH)], r_raw.at[z_lo, c * SUB + i],
                                r_src.at[n, i], r_recv.at[z_lo, c * SUB + i],
                                device(xh, xl, y, at_z(q), half)))

    def own_copy(i):
        return pltpu.make_async_copy(d_ref.at[:, pl.ds(i * WIDTH, WIDTH)], r_raw.at[z_lo, c * SUB + i],
                                     r_recv.at[z_lo, c * SUB + i])

    def own_send(i):
        return pltpu.make_async_remote_copy(
            src_ref=d_ref.at[:, pl.ds(i * WIDTH, WIDTH)], dst_ref=r_raw.at[z_lo, c * SUB + i],
            send_sem=r_src.at[2, i], recv_sem=r_recv.at[z_lo, c * SUB + i],
            device_id=device(xh, xl, y, z, other), device_id_type=MESH)

    for i in range(SUB):
        @pl.when(half == c)
        def _():
            own_copy(i).start()

        @pl.when(half != c)
        def _():
            own_send(i).start()

    for k in range(1, 8):
        g = (me + k) % 8
        started.append(send(d_ref, q_raw.at[me, c], q_send.at[k], q_recv.at[me, c],
                            device(xh, g // NY, g % NY, z, c)))
    started.append(send(d_ref, q_raw.at[me, c], q_send.at[0], q_recv.at[me, c], device(xh, xl, y, z, other)))

    def pass_on(sign, s, most):
        origin = at_z(-sign * s)
        lo = origin % 8

        @pl.when((origin // 8 == c) & (s < most))
        def _():
            for j in range(PIECES):
                arrived(r_raw.at[lo, j], r_recv.at[lo, j])
                send(r_raw.at[lo, j], r_raw.at[lo, j], r_send.at[lo, j], r_recv.at[lo, j],
                     device(xh, xl, y, at_z(sign), c))

        @pl.when((origin // 8 == c) & (s == most))
        def _():
            for j in range(PIECES):
                arrived(r_raw.at[lo, j], r_recv.at[lo, j])

    def pass_both(s):
        pass_on(1, s, 8)
        pass_on(-1, s, 7)

    pass_both(1)

    for n in range(len(NEAR)):
        arrived(z_near.at[n], zn_recv.at[n])
    up = {k: n for n, k in enumerate(NEAR)}

    def gathered(ks):
        whole = stat[...]
        for k in ks:
            whole = whole + z_near[up[k]]
        return whole

    z_out[0] = gathered((-1, 1, 2))
    z_out[1] = gathered((-2, -1, 1, 2))
    for n, k in enumerate((FAR, -FAR)):
        started.append(send(z_out.at[n], z_far.at[n], zf_send.at[n], zf_recv.at[n], device(xh, xl, y, at_z(k), c)))

    pass_both(2)
    pass_both(3)
    for n in range(2):
        arrived(z_far.at[n], zf_recv.at[n])
    p_stat[me, c] = gathered(NEAR) + z_far[0] + z_far[1]

    for k in range(1, 8):
        g = (me + k) % 8
        for cc in range(2):
            started.append(send(p_stat.at[me, c], p_stat.at[me, c], ps_send.at[k, cc], ps_recv.at[me, c],
                                device(xh, g // NY, g % NY, z, (c + cc) % 2)))
    started.append(send(p_stat.at[me, c], p_stat.at[me, c], ps_send.at[0, 0], ps_recv.at[me, c],
                        device(xh, xl, y, z, other)))
    for k in range(1, 8):
        g = (me + k) % 8
        arrived(q_raw.at[g, c], q_recv.at[g, c])
        started.append(send(q_raw.at[g, c], q_raw.at[g, c], q_send.at[8 + k], q_recv.at[g, c],
                            device(xh, xl, y, z, other)))
    pass_both(4)
    pass_both(5)
    for k in range(8):
        g = (me + k) % 8
        for cc in range(2):
            o = (c + cc) % 2
            if k or cc:
                arrived(p_stat.at[g, o], ps_recv.at[g, o])
    wholes = []
    for o in range(2):
        whole = p_stat[0, o]
        for g in range(1, 8):
            whole = whole + p_stat[g, o]
        wholes.append(whole)
        mean[:, o * COLS:(o + 1) * COLS] = whole[:, 0:COLS] / total
    mine = jnp.where(c == 0, wholes[0], wholes[1])
    upd_ref[...] = (mine[:, COLS:2 * COLS] - (mine[:, 0:COLS] / total) * mine[:, 2 * COLS:2 * COLS + 1]) * factor

    def center(raw, columns):
        return ((raw.astype(F32) - mean[:, columns]) * factor).astype(BF16)

    here, there = (pl.ds(pl.multiple_of(o * COLS, COLS), COLS) for o in (c, other))
    q_c[pl.ds(me * ROWS, ROWS), here] = center(d_ref[...], here)
    arrived(q_raw.at[me, other], q_recv.at[me, other])
    q_c[pl.ds(me * ROWS, ROWS), there] = center(q_raw[me, other], there)
    for k in range(1, 8):
        g = (me + k) % 8
        arrived(q_raw.at[g, other], q_recv.at[g, other])
        for o in range(2):
            q_c[pl.ds(g * ROWS, ROWS), o * COLS:(o + 1) * COLS] = center(q_raw[g, o], slice(o * COLS, (o + 1) * COLS))

    @pl.when(half == c)
    def _():
        for j in range(PIECES):
            arrived(r_raw.at[z_lo, j], r_recv.at[z_lo, j])

    slot = xh * NY + y

    def out_is_me(g):
        return same & (g == me)

    def group_at(t):
        most = LOOP_FROM
        for v in range(4):
            up_steps = (z - (c * 8 + t * 4 + v) + NZ) % NZ
            most = jnp.maximum(most, jnp.minimum(up_steps, NZ - up_steps))
        return most

    def product(t):
        for v in range(4):
            for j in range(PIECES):
                r_c[v * ROWS:(v + 1) * ROWS, j * WIDTH:(j + 1) * WIDTH] = center(
                    r_raw[t * 4 + v, j], slice(j * WIDTH, (j + 1) * WIDTH))
        for u in range(4):
            part = lax.dot_general(q_c[u * 160:(u + 1) * 160, :], r_c[...], (((1,), (1,)), ((), ())),
                                   preferred_element_type=F32).astype(BF16)
            for g in (2 * u, 2 * u + 1):
                p_out[t, g] = part[(g - 2 * u) * ROWS:(g - 2 * u + 1) * ROWS]

                @pl.when(out_is_me(g))
                def _():
                    pltpu.make_async_copy(p_out.at[t, g], p_in.at[t, slot], o_recv.at[t, slot]).start()

                @pl.when(jnp.logical_not(out_is_me(g)))
                def _():
                    send(p_out.at[t, g], p_in.at[t, slot], o_send.at[t, g], o_recv.at[t, slot],
                         device(xl, g // NY, g % NY, z, c))

    def step(s, carry):
        @pl.when(s > LOOP_FROM)
        def _():
            pass_both(s)

        def one(t, inner):
            @pl.when(group_at(t) == s)
            def _():
                product(t)
            return inner

        return lax.fori_loop(0, 2, one, carry)

    lax.fori_loop(LOOP_FROM, 9, step, 0)

    first = (group_at(1) < group_at(0)).astype(jnp.int32)

    def assemble(n, carry):
        t = jnp.where(n == 0, first, 1 - first)
        for k in range(8):
            arrived(p_in.at[t, k], o_recv.at[t, k])
        for u in range(5):
            rows = slice(u * 16, (u + 1) * 16)
            added = [p_in[t, k, rows].astype(F32) + p_in[t, NY + k, rows].astype(F32) for k in range(NY)]
            for w in range(2):
                gram_ref[rows, pl.ds(pl.multiple_of(t * 1280 + w * 640, 640), 640)] = jnp.concatenate(
                    [added[k][:, (2 * w + v) * ROWS:(2 * w + v + 1) * ROWS] for v in range(2) for k in range(NY)],
                    axis=1)
        return carry

    lax.fori_loop(0, 2, assemble, 0)

    for copy in started:
        copy.wait_send()
    for i in range(SUB):
        @pl.when(half != c)
        def _():
            own_send(i).wait_send()
    for sign, most in ((1, 8), (-1, 7)):
        for s in range(1, most):
            origin = at_z(-sign * s)

            @pl.when(origin // 8 == c)
            def _():
                for j in range(PIECES):
                    handle(r_raw.at[origin % 8, j], r_send.at[origin % 8, j]).wait_send()
    for t in range(2):
        for g in range(8):
            @pl.when(jnp.logical_not(out_is_me(g)))
            def _():
                handle(p_out.at[t, g], o_send.at[t, g]).wait_send()


def shards(derivatives, epsilon):
    total = derivatives.shape[0] * 128
    dma = pltpu.SemaphoreType.DMA
    gram, upd = pl.pallas_call(
        functools.partial(kernel, total),
        name="gram",
        out_shape=(jax.ShapeDtypeStruct((ROWS, 2560), F32), jax.ShapeDtypeStruct((1, COLS), F32)),
        in_specs=[pl.BlockSpec(memory_space=pl.ANY), pl.BlockSpec(memory_space=pltpu.VMEM)],
        out_specs=[pl.BlockSpec(memory_space=pltpu.VMEM)] * 2,
        scratch_shapes=[
            pltpu.VMEM((ROWS, COLS), BF16),
            pltpu.VMEM((8, 2, ROWS, COLS), BF16),
            pltpu.VMEM((8, PIECES, ROWS, WIDTH), BF16),
            pltpu.VMEM((640, 2 * COLS), BF16),
            pltpu.VMEM((GROUP, 2 * COLS), BF16),
            pltpu.VMEM((1, STAT), F32),
            pltpu.VMEM((len(NEAR), 1, STAT), F32),
            pltpu.VMEM((2, 1, STAT), F32),
            pltpu.VMEM((2, 1, STAT), F32),
            pltpu.VMEM((8, 2, 1, STAT), F32),
            pltpu.VMEM((1, 2 * COLS), F32),
            pltpu.VMEM((2, 8, ROWS, GROUP), BF16),
            pltpu.VMEM((2, 8, ROWS, GROUP), BF16),
            dma,
            dma((16,)), dma((8, 2)),
            dma((3, SUB)), dma((8, PIECES)), dma((8, PIECES)),
            dma((len(NEAR),)), dma((len(NEAR),)), dma((2,)), dma((2,)),
            dma((8, 2)), dma((8, 2)),
            dma((2, 8)), dma((2, 8)),
        ],
        compiler_params=pltpu.CompilerParams(collective_id=0, has_side_effects=True, vmem_limit_bytes=24 << 20),
    )(derivatives, epsilon.reshape(1, ROWS))
    return gram, upd.reshape(COLS)


def solution(mesh):
    in_specs = (P("smp", "par"), P("smp"))
    out_specs = (P("smp", "par"), P("par"))
    return jax.shard_map(shards, mesh=mesh, in_specs=in_specs, out_specs=out_specs, check_vma=False)
```

```python
import functools
import math

import jax
import jax.numpy as jnp
from jax import lax
from jax.experimental import pallas as pl
from jax.experimental.pallas import tpu as pltpu
from jax.sharding import PartitionSpec as P

MESH = pl.DeviceIdType.MESH
F32, BF16 = jnp.float32, jnp.bfloat16
ROWS, COLS = 80, 512
NZ, NY = 16, 4
SUB = 2
WIDTH = COLS // SUB
PIECES = 2 * SUB
SPLIT = 256
STAT = 2 * COLS + 128
NEAR = (1, -1, 2, -2, 3, -3)
FAR = 6
LOOP_FROM = 5


def device(xh, xl, y, z, c):
    return (xl * 64 + z * NY + y, xh * 2 + c)


def kernel(total, d_hbm, eps_ref, gram_ref, upd_ref,
           d_ref, q_raw, r_raw, q_c, r_c, stat, z_near, z_out, z_far, p_stat, mean, p_out0, p_out1, p_in0, p_in1,
           d_sem, q_own, q_send, q_recv, r_src, r_send, r_recv, zn_send, zn_recv, zf_send, zf_recv,
           ps_send, ps_recv, o_send, o_recv):
    s_at, p_at = lax.axis_index("smp"), lax.axis_index("par")
    xl, z, y = s_at // 64, (s_at // NY) % NZ, s_at % NY
    xh, c = p_at // 2, p_at % 2
    other = 1 - c
    half, z_lo = z // 8, z % 8
    me = xl * NY + y
    factor = 1.0 / math.sqrt(total)
    load = pltpu.make_async_copy(d_hbm, d_ref, d_sem)
    load.start()

    def at_z(step):
        return (z + step + NZ) % NZ

    barrier = pltpu.get_barrier_semaphore()

    def greet(where):
        pl.semaphore_signal(barrier, inc=1, device_id=where, device_id_type=MESH)

    same = (xl == xh)
    for k in range(8):
        src_xh, src_y = k // NY, k % NY

        @pl.when(jnp.logical_not(same & (src_xh == xh) & (src_y == y)))
        def _():
            greet(device(src_xh, xh, src_y, z, c))

    for k in NEAR:
        greet(device(xh, xl, y, at_z(k), c))
    for k in (1, -1):
        greet(device(xh, xl, y, at_z(k), other))
    for k in range(1, 8):
        g = (me + k) % 8
        for cc in range(2):
            greet(device(xh, g // NY, g % NY, z, cc))
    greet(device(xh, xl, y, z, other))

    load.wait()
    d = d_ref[...].astype(F32)
    eps = eps_ref[...]
    stat[:, 0:COLS] = jnp.sum(d, axis=0, keepdims=True)
    stat[:, COLS:2 * COLS] = lax.dot_general(
        eps, d, (((1,), (0,)), ((), ())), precision=lax.Precision.HIGHEST, preferred_element_type=F32)
    stat[:, 2 * COLS:] = jnp.broadcast_to(jnp.sum(eps, axis=1, keepdims=True), (1, 128))

    pl.semaphore_wait(barrier, 8 - same.astype(jnp.int32) + len(NEAR) + 2 + 14 + 1)

    started = []

    def send(src, dst, s_sem, r_sem, where):
        copy = pltpu.make_async_remote_copy(src_ref=src, dst_ref=dst, send_sem=s_sem, recv_sem=r_sem,
                                            device_id=where, device_id_type=MESH)
        copy.start()
        return copy

    def handle(ref, sem):
        return pltpu.make_async_remote_copy(src_ref=ref, dst_ref=ref, send_sem=sem, recv_sem=sem,
                                            device_id=(s_at, p_at), device_id_type=MESH)

    def arrived(ref, sem):
        handle(ref, sem).wait_recv()

    for n, k in enumerate(NEAR):
        started.append(send(stat, z_near.at[n], zn_send.at[n], zn_recv.at[n], device(xh, xl, y, at_z(-k), c)))

    for i in range(SUB):
        for n, q in enumerate((1, -1)):
            started.append(send(d_ref.at[:, pl.ds(i * WIDTH, WIDTH)], r_raw.at[z_lo, c * SUB + i],
                                r_src.at[n, i], r_recv.at[z_lo, c * SUB + i],
                                device(xh, xl, y, at_z(q), half)))

    def own_copy(i):
        return pltpu.make_async_copy(d_ref.at[:, pl.ds(i * WIDTH, WIDTH)], r_raw.at[z_lo, c * SUB + i],
                                     r_recv.at[z_lo, c * SUB + i])

    def own_send(i):
        return pltpu.make_async_remote_copy(
            src_ref=d_ref.at[:, pl.ds(i * WIDTH, WIDTH)], dst_ref=r_raw.at[z_lo, c * SUB + i],
            send_sem=r_src.at[2, i], recv_sem=r_recv.at[z_lo, c * SUB + i],
            device_id=device(xh, xl, y, z, other), device_id_type=MESH)

    for i in range(SUB):
        @pl.when(half == c)
        def _():
            own_copy(i).start()

        @pl.when(half != c)
        def _():
            own_send(i).start()

    own_here = pltpu.make_async_copy(d_ref, q_raw.at[me, c], q_own)
    own_here.start()

    for k in range(1, 8):
        g = (me + k) % 8
        started.append(send(d_ref, q_raw.at[me, c], q_send.at[k], q_recv.at[me, c],
                            device(xh, g // NY, g % NY, z, c)))
    started.append(send(d_ref, q_raw.at[me, c], q_send.at[0], q_recv.at[me, c], device(xh, xl, y, z, other)))

    def pass_on(sign, s, most):
        origin = at_z(-sign * s)
        lo = origin % 8

        @pl.when((origin // 8 == c) & (s < most))
        def _():
            for j in range(PIECES):
                arrived(r_raw.at[lo, j], r_recv.at[lo, j])
                send(r_raw.at[lo, j], r_raw.at[lo, j], r_send.at[lo, j], r_recv.at[lo, j],
                     device(xh, xl, y, at_z(sign), c))

        @pl.when((origin // 8 == c) & (s == most))
        def _():
            for j in range(PIECES):
                arrived(r_raw.at[lo, j], r_recv.at[lo, j])

    def pass_both(s):
        pass_on(1, s, 8)
        pass_on(-1, s, 7)

    pass_both(1)

    for n in range(len(NEAR)):
        arrived(z_near.at[n], zn_recv.at[n])
    up = {k: n for n, k in enumerate(NEAR)}

    def gathered(ks):
        whole = stat[...]
        for k in ks:
            whole = whole + z_near[up[k]]
        return whole

    z_out[0] = gathered((-1, 1, 2))
    z_out[1] = gathered((-2, -1, 1, 2))
    for n, k in enumerate((FAR, -FAR)):
        started.append(send(z_out.at[n], z_far.at[n], zf_send.at[n], zf_recv.at[n], device(xh, xl, y, at_z(k), c)))

    pass_both(2)
    pass_both(3)
    for n in range(2):
        arrived(z_far.at[n], zf_recv.at[n])
    p_stat[me, c] = gathered(NEAR) + z_far[0] + z_far[1]

    for k in range(1, 8):
        g = (me + k) % 8
        for cc in range(2):
            started.append(send(p_stat.at[me, c], p_stat.at[me, c], ps_send.at[k, cc], ps_recv.at[me, c],
                                device(xh, g // NY, g % NY, z, (c + cc) % 2)))
    started.append(send(p_stat.at[me, c], p_stat.at[me, c], ps_send.at[0, 0], ps_recv.at[me, c],
                        device(xh, xl, y, z, other)))
    for k in range(1, 8):
        g = (me + k) % 8
        arrived(q_raw.at[g, c], q_recv.at[g, c])
        started.append(send(q_raw.at[g, c], q_raw.at[g, c], q_send.at[8 + k], q_recv.at[g, c],
                            device(xh, xl, y, z, other)))
    pass_both(4)
    pass_both(5)
    for k in range(8):
        g = (me + k) % 8
        for cc in range(2):
            o = (c + cc) % 2
            if k or cc:
                arrived(p_stat.at[g, o], ps_recv.at[g, o])
    wholes = []
    for o in range(2):
        whole = p_stat[0, o]
        for g in range(1, 8):
            whole = whole + p_stat[g, o]
        wholes.append(whole)
        mean[:, o * COLS:(o + 1) * COLS] = whole[:, 0:COLS] / total
    mine = jnp.where(c == 0, wholes[0], wholes[1])
    upd_ref[...] = (mine[:, COLS:2 * COLS] - (mine[:, 0:COLS] / total) * mine[:, 2 * COLS:2 * COLS + 1]) * factor

    def center(raw, columns):
        return ((raw.astype(F32) - mean[:, columns]) * factor).astype(BF16)

    for k in range(8):
        g = (me + k) % 8
        if k:
            arrived(q_raw.at[g, other], q_recv.at[g, other])
        else:
            own_here.wait()
            arrived(q_raw.at[me, other], q_recv.at[me, other])

    def center_pair(u):
        for v in range(2):
            for o in range(2):
                q_c[pl.ds(u * 160 + v * ROWS, ROWS), o * COLS:(o + 1) * COLS] = center(
                    q_raw[2 * u + v, o], slice(o * COLS, (o + 1) * COLS))

    @pl.when(half == c)
    def _():
        for j in range(PIECES):
            arrived(r_raw.at[z_lo, j], r_recv.at[z_lo, j])

    slot = xh * NY + y
    outs = ((p_out0, p_in0, slice(0, SPLIT), range(4)), (p_out1, p_in1, slice(SPLIT, 640), range(3, 8)))

    def out_is_me(g):
        return same & (g == me)

    def ready_at(los):
        most = LOOP_FROM
        for v in los:
            up_steps = (z - (c * 8 + v) + NZ) % NZ
            most = jnp.maximum(most, jnp.minimum(up_steps, NZ - up_steps))
        return most

    ready = [ready_at(outs[t][3]) for t in range(2)]
    early = jnp.minimum(ready[0], ready[1]) == LOOP_FROM
    leads = (ready[0] <= ready[1], ready[1] < ready[0])
    turn = y + 2 * xh

    @pl.when(jnp.logical_not(early))
    def _():
        for u in range(4):
            center_pair(u)

    def product(t):
        p_out, p_in, columns, los = outs[t]
        for v in los:
            for j in range(PIECES):
                r_c[v * ROWS:(v + 1) * ROWS, j * WIDTH:(j + 1) * WIDTH] = center(
                    r_raw[v, j], slice(j * WIDTH, (j + 1) * WIDTH))
        for i in range(4):
            u = (turn + i) % 4

            @pl.when(early & leads[t])
            def _():
                center_pair(u)

            part = lax.dot_general(q_c[pl.ds(u * 160, 160), :], r_c[columns, :], (((1,), (1,)), ((), ())),
                                   preferred_element_type=F32).astype(BF16)
            for v in range(2):
                g = 2 * u + v
                p_out[g] = part[v * ROWS:(v + 1) * ROWS]

                @pl.when(out_is_me(g))
                def _():
                    pltpu.make_async_copy(p_out.at[g], p_in.at[slot], o_recv.at[t, slot]).start()

                @pl.when(jnp.logical_not(out_is_me(g)))
                def _():
                    send(p_out.at[g], p_in.at[slot], o_send.at[t, g], o_recv.at[t, slot],
                         device(xl, g // NY, g % NY, z, c))

    def step(s, carry):
        @pl.when(s > LOOP_FROM)
        def _():
            pass_both(s)

        for t in range(2):
            @pl.when(ready[t] == s)
            def _():
                product(t)
        return carry

    lax.fori_loop(LOOP_FROM, 9, step, 0)

    for copy in started:
        copy.wait_send()
    for i in range(SUB):
        @pl.when(half != c)
        def _():
            own_send(i).wait_send()
    for sign, most in ((1, 8), (-1, 7)):
        for s in range(1, most):
            origin = at_z(-sign * s)

            @pl.when(origin // 8 == c)
            def _():
                for j in range(PIECES):
                    handle(r_raw.at[origin % 8, j], r_send.at[origin % 8, j]).wait_send()
    for t in range(2):
        for g in range(8):
            @pl.when(jnp.logical_not(out_is_me(g)))
            def _():
                handle(outs[t][0].at[g], o_send.at[t, g]).wait_send()

    for t in range(2):
        for k in range(8):
            arrived(outs[t][1].at[k], o_recv.at[t, k])
    for u in range(5):
        rows = slice(u * 16, (u + 1) * 16)
        added = [jnp.concatenate([p_in[k, rows].astype(F32) + p_in[NY + k, rows].astype(F32)
                                  for p_in in (p_in0, p_in1)], axis=1) for k in range(NY)]
        for w in range(4):
            gram_ref[rows, w * 640:(w + 1) * 640] = jnp.concatenate(
                [added[k][:, (2 * w + v) * ROWS:(2 * w + v + 1) * ROWS] for v in range(2) for k in range(NY)], axis=1)


def shards(derivatives, epsilon):
    total = derivatives.shape[0] * 128
    dma = pltpu.SemaphoreType.DMA
    gram, upd = pl.pallas_call(
        functools.partial(kernel, total),
        name="gram",
        out_shape=(jax.ShapeDtypeStruct((ROWS, 2560), F32), jax.ShapeDtypeStruct((1, COLS), F32)),
        in_specs=[pl.BlockSpec(memory_space=pl.ANY), pl.BlockSpec(memory_space=pltpu.VMEM)],
        out_specs=[pl.BlockSpec(memory_space=pltpu.VMEM)] * 2,
        scratch_shapes=[
            pltpu.VMEM((ROWS, COLS), BF16),
            pltpu.VMEM((8, 2, ROWS, COLS), BF16),
            pltpu.VMEM((8, PIECES, ROWS, WIDTH), BF16),
            pltpu.VMEM((640, 2 * COLS), BF16),
            pltpu.VMEM((640, 2 * COLS), BF16),
            pltpu.VMEM((1, STAT), F32),
            pltpu.VMEM((len(NEAR), 1, STAT), F32),
            pltpu.VMEM((2, 1, STAT), F32),
            pltpu.VMEM((2, 1, STAT), F32),
            pltpu.VMEM((8, 2, 1, STAT), F32),
            pltpu.VMEM((1, 2 * COLS), F32),
            pltpu.VMEM((8, ROWS, SPLIT), BF16),
            pltpu.VMEM((8, ROWS, 640 - SPLIT), BF16),
            pltpu.VMEM((8, ROWS, SPLIT), BF16),
            pltpu.VMEM((8, ROWS, 640 - SPLIT), BF16),
            dma, dma,
            dma((16,)), dma((8, 2)),
            dma((3, SUB)), dma((8, PIECES)), dma((8, PIECES)),
            dma((len(NEAR),)), dma((len(NEAR),)), dma((2,)), dma((2,)),
            dma((8, 2)), dma((8, 2)),
            dma((2, 8)), dma((2, 8)),
        ],
        compiler_params=pltpu.CompilerParams(collective_id=0, has_side_effects=True, vmem_limit_bytes=24 << 20),
    )(derivatives, epsilon.reshape(1, ROWS))
    return gram, upd.reshape(COLS)


def solution(mesh):
    in_specs = (P("smp", "par"), P("smp"))
    out_specs = (P("smp", "par"), P("par"))
    return jax.shard_map(shards, mesh=mesh, in_specs=in_specs, out_specs=out_specs, check_vma=False)
```

```python
import functools
import math

import jax
import jax.numpy as jnp
from jax import lax
from jax.experimental import pallas as pl
from jax.experimental.pallas import tpu as pltpu
from jax.sharding import PartitionSpec as P

MESH = pl.DeviceIdType.MESH
F32, BF16 = jnp.float32, jnp.bfloat16
ROWS, COLS = 80, 512
NZ, NY = 16, 4
SUB = 4
WIDTH = COLS // SUB
PIECES = 2 * SUB
SPLIT = 256
STAT = 2 * COLS + 128
NEAR = (1, -1, 2, -2, 3, -3)
FAR = 6
LOOP_FROM = 5
ASSEMBLE_VMEM = 16 << 20


def device(xh, xl, y, z, c):
    return (xl * 64 + z * NY + y, xh * 2 + c)


def kernel(total, d_hbm, eps_ref, p_in0, p_in1, upd_ref,
           d_ref, q_raw, r_raw, q_c, r_c, stat, z_near, z_out, z_far, p_stat, mean, p_out0, p_out1,
           d_sem, q_own, q_send, q_recv, r_src, r_send, r_recv, zn_send, zn_recv, zf_send, zf_recv,
           ps_send, ps_recv, o_send, o_recv):
    s_at, p_at = lax.axis_index("smp"), lax.axis_index("par")
    xl, z, y = s_at // 64, (s_at // NY) % NZ, s_at % NY
    xh, c = p_at // 2, p_at % 2
    other = 1 - c
    half, z_lo = z // 8, z % 8
    me = xl * NY + y
    factor = 1.0 / math.sqrt(total)
    load = pltpu.make_async_copy(d_hbm, d_ref, d_sem)
    load.start()

    def at_z(step):
        return (z + step + NZ) % NZ

    barrier = pltpu.get_barrier_semaphore()

    def greet(where):
        pl.semaphore_signal(barrier, inc=1, device_id=where, device_id_type=MESH)

    same = (xl == xh)
    for k in range(8):
        src_xh, src_y = k // NY, k % NY

        @pl.when(jnp.logical_not(same & (src_xh == xh) & (src_y == y)))
        def _():
            greet(device(src_xh, xh, src_y, z, c))

    for k in NEAR:
        greet(device(xh, xl, y, at_z(k), c))
    for k in (1, -1):
        greet(device(xh, xl, y, at_z(k), other))
    for k in range(1, 8):
        g = (me + k) % 8
        for cc in range(2):
            greet(device(xh, g // NY, g % NY, z, cc))
    greet(device(xh, xl, y, z, other))

    load.wait()
    d = d_ref[...].astype(F32)
    eps = eps_ref[...]
    stat[:, 0:COLS] = jnp.sum(d, axis=0, keepdims=True)
    stat[:, COLS:2 * COLS] = lax.dot_general(
        eps, d, (((1,), (0,)), ((), ())), precision=lax.Precision.HIGHEST, preferred_element_type=F32)
    stat[:, 2 * COLS:] = jnp.broadcast_to(jnp.sum(eps, axis=1, keepdims=True), (1, 128))

    pl.semaphore_wait(barrier, 8 - same.astype(jnp.int32) + len(NEAR) + 2 + 14 + 1)

    started = []

    def send(src, dst, s_sem, r_sem, where):
        copy = pltpu.make_async_remote_copy(src_ref=src, dst_ref=dst, send_sem=s_sem, recv_sem=r_sem,
                                            device_id=where, device_id_type=MESH)
        copy.start()
        return copy

    def handle(ref, sem):
        return pltpu.make_async_remote_copy(src_ref=ref, dst_ref=ref, send_sem=sem, recv_sem=sem,
                                            device_id=(s_at, p_at), device_id_type=MESH)

    def arrived(ref, sem):
        handle(ref, sem).wait_recv()

    for n, k in enumerate(NEAR):
        started.append(send(stat, z_near.at[n], zn_send.at[n], zn_recv.at[n], device(xh, xl, y, at_z(-k), c)))

    for i in range(SUB):
        for n, q in enumerate((1, -1)):
            started.append(send(d_ref.at[:, pl.ds(i * WIDTH, WIDTH)], r_raw.at[z_lo, c * SUB + i],
                                r_src.at[n, i], r_recv.at[z_lo, c * SUB + i],
                                device(xh, xl, y, at_z(q), half)))

    def own_copy(i):
        return pltpu.make_async_copy(d_ref.at[:, pl.ds(i * WIDTH, WIDTH)], r_raw.at[z_lo, c * SUB + i],
                                     r_recv.at[z_lo, c * SUB + i])

    def own_send(i):
        return pltpu.make_async_remote_copy(
            src_ref=d_ref.at[:, pl.ds(i * WIDTH, WIDTH)], dst_ref=r_raw.at[z_lo, c * SUB + i],
            send_sem=r_src.at[2, i], recv_sem=r_recv.at[z_lo, c * SUB + i],
            device_id=device(xh, xl, y, z, other), device_id_type=MESH)

    for i in range(SUB):
        @pl.when(half == c)
        def _():
            own_copy(i).start()

        @pl.when(half != c)
        def _():
            own_send(i).start()

    own_here = pltpu.make_async_copy(d_ref, q_raw.at[me, c], q_own)
    own_here.start()

    for k in range(1, 8):
        g = (me + k) % 8
        started.append(send(d_ref, q_raw.at[me, c], q_send.at[k], q_recv.at[me, c],
                            device(xh, g // NY, g % NY, z, c)))
    started.append(send(d_ref, q_raw.at[me, c], q_send.at[0], q_recv.at[me, c], device(xh, xl, y, z, other)))

    def pass_both(s):
        ways = [(sign, most, at_z(-sign * s)) for sign, most in ((1, 8), (-1, 7))]
        for j in range(PIECES):
            for sign, most, origin in ways:
                lo = origin % 8

                @pl.when((origin // 8 == c) & (s <= most))
                def _():
                    arrived(r_raw.at[lo, j], r_recv.at[lo, j])

                    @pl.when(s < most)
                    def _():
                        send(r_raw.at[lo, j], r_raw.at[lo, j], r_send.at[lo, j], r_recv.at[lo, j],
                             device(xh, xl, y, at_z(sign), c))

    pass_both(1)

    for n in range(len(NEAR)):
        arrived(z_near.at[n], zn_recv.at[n])
    up = {k: n for n, k in enumerate(NEAR)}

    def gathered(ks):
        whole = stat[...]
        for k in ks:
            whole = whole + z_near[up[k]]
        return whole

    z_out[0] = gathered((-1, 1, 2))
    z_out[1] = gathered((-2, -1, 1, 2))
    for n, k in enumerate((FAR, -FAR)):
        started.append(send(z_out.at[n], z_far.at[n], zf_send.at[n], zf_recv.at[n], device(xh, xl, y, at_z(k), c)))

    pass_both(2)
    pass_both(3)
    for n in range(2):
        arrived(z_far.at[n], zf_recv.at[n])
    p_stat[me, c] = gathered(NEAR) + z_far[0] + z_far[1]

    for k in range(1, 8):
        g = (me + k) % 8
        for cc in range(2):
            started.append(send(p_stat.at[me, c], p_stat.at[me, c], ps_send.at[k, cc], ps_recv.at[me, c],
                                device(xh, g // NY, g % NY, z, (c + cc) % 2)))
    started.append(send(p_stat.at[me, c], p_stat.at[me, c], ps_send.at[0, 0], ps_recv.at[me, c],
                        device(xh, xl, y, z, other)))
    pass_both(4)
    for k in range(1, 8):
        g = (me + k) % 8
        arrived(q_raw.at[g, c], q_recv.at[g, c])
        started.append(send(q_raw.at[g, c], q_raw.at[g, c], q_send.at[8 + k], q_recv.at[g, c],
                            device(xh, xl, y, z, other)))
    pass_both(5)
    for k in range(8):
        g = (me + k) % 8
        for cc in range(2):
            o = (c + cc) % 2
            if k or cc:
                arrived(p_stat.at[g, o], ps_recv.at[g, o])
    wholes = []
    for o in range(2):
        whole = p_stat[0, o]
        for g in range(1, 8):
            whole = whole + p_stat[g, o]
        wholes.append(whole)
        mean[:, o * COLS:(o + 1) * COLS] = whole[:, 0:COLS] / total
    mine = jnp.where(c == 0, wholes[0], wholes[1])
    upd_ref[...] = (mine[:, COLS:2 * COLS] - (mine[:, 0:COLS] / total) * mine[:, 2 * COLS:2 * COLS + 1]) * factor

    def center(raw, columns):
        return ((raw.astype(F32) - mean[:, columns]) * factor).astype(BF16)

    for k in range(8):
        g = (me + k) % 8
        if k:
            arrived(q_raw.at[g, other], q_recv.at[g, other])
        else:
            own_here.wait()
            arrived(q_raw.at[me, other], q_recv.at[me, other])

    def center_pair(u):
        for v in range(2):
            for o in range(2):
                q_c[pl.ds(u * 160 + v * ROWS, ROWS), o * COLS:(o + 1) * COLS] = center(
                    q_raw[2 * u + v, o], slice(o * COLS, (o + 1) * COLS))

    @pl.when(half == c)
    def _():
        for j in range(PIECES):
            arrived(r_raw.at[z_lo, j], r_recv.at[z_lo, j])

    slot = xh * NY + y
    outs = ((p_out0, p_in0, slice(0, SPLIT), range(4)), (p_out1, p_in1, slice(SPLIT, 640), range(3, 8)))

    def out_is_me(g):
        return same & (g == me)

    def ready_at(los):
        most = LOOP_FROM
        for v in los:
            up_steps = (z - (c * 8 + v) + NZ) % NZ
            most = jnp.maximum(most, jnp.minimum(up_steps, NZ - up_steps))
        return most

    ready = [ready_at(outs[t][3]) for t in range(2)]
    early = jnp.minimum(ready[0], ready[1]) == LOOP_FROM
    leads = (ready[0] <= ready[1], ready[1] < ready[0])
    turn = y + 2 * xh

    @pl.when(jnp.logical_not(early))
    def _():
        for u in range(4):
            center_pair(u)

    def product(t, part_at):
        p_out, p_in, columns, los = outs[t]
        for v in los if part_at == 0 else ():
            for j in range(PIECES):
                r_c[v * ROWS:(v + 1) * ROWS, j * WIDTH:(j + 1) * WIDTH] = center(
                    r_raw[v, j], slice(j * WIDTH, (j + 1) * WIDTH))
        for i in range(2 * part_at, 2 * part_at + 2):
            u = (turn + i) % 4

            @pl.when(early & leads[t])
            def _():
                center_pair(u)

            part = lax.dot_general(q_c[pl.ds(u * 160, 160), :], r_c[columns, :], (((1,), (1,)), ((), ())),
                                   preferred_element_type=F32).astype(BF16)
            for v in range(2):
                g = 2 * u + v
                p_out[g] = part[v * ROWS:(v + 1) * ROWS]

                @pl.when(out_is_me(g))
                def _():
                    pltpu.make_async_copy(p_out.at[g], p_in.at[slot], o_recv.at[t, slot]).start()

                @pl.when(jnp.logical_not(out_is_me(g)))
                def _():
                    send(p_out.at[g], p_in.at[slot], o_send.at[t, g], o_recv.at[t, slot],
                         device(xl, g // NY, g % NY, z, c))

    def step(s, carry):
        @pl.when(s > LOOP_FROM)
        def _():
            pass_both(s)

        for t in range(2):
            for part_at in range(2):
                @pl.when(jnp.minimum(ready[t] + part_at, 8) == s)
                def _():
                    product(t, part_at)
        return carry

    lax.fori_loop(LOOP_FROM, 9, step, 0)

    for copy in started:
        copy.wait_send()
    for i in range(SUB):
        @pl.when(half != c)
        def _():
            own_send(i).wait_send()
    for sign, most in ((1, 8), (-1, 7)):
        for s in range(1, most):
            origin = at_z(-sign * s)

            @pl.when(origin // 8 == c)
            def _():
                for j in range(PIECES):
                    handle(r_raw.at[origin % 8, j], r_send.at[origin % 8, j]).wait_send()
    for t in range(2):
        for g in range(8):
            @pl.when(jnp.logical_not(out_is_me(g)))
            def _():
                handle(outs[t][0].at[g], o_send.at[t, g]).wait_send()

    for t in range(2):
        for k in range(8):
            arrived(outs[t][1].at[k], o_recv.at[t, k])


def assemble(p_in0, p_in1, upd_in, gram_ref, upd_ref):
    upd_ref[...] = upd_in[...]
    for u in range(5):
        rows = slice(u * 16, (u + 1) * 16)
        added = [jnp.concatenate([p_in[k, rows].astype(F32) + p_in[NY + k, rows].astype(F32)
                                  for p_in in (p_in0, p_in1)], axis=1) for k in range(NY)]
        for w in range(4):
            gram_ref[rows, w * 640:(w + 1) * 640] = jnp.concatenate(
                [added[k][:, (2 * w + v) * ROWS:(2 * w + v + 1) * ROWS] for v in range(2) for k in range(NY)], axis=1)


def shards(derivatives, epsilon):
    total = derivatives.shape[0] * 128
    dma = pltpu.SemaphoreType.DMA
    parts0, parts1, upd = pl.pallas_call(
        functools.partial(kernel, total),
        name="gram",
        out_shape=(jax.ShapeDtypeStruct((8, ROWS, SPLIT), BF16), jax.ShapeDtypeStruct((8, ROWS, 640 - SPLIT), BF16),
                   jax.ShapeDtypeStruct((1, COLS), F32)),
        in_specs=[pl.BlockSpec(memory_space=pl.ANY), pl.BlockSpec(memory_space=pltpu.VMEM)],
        out_specs=[pl.BlockSpec(memory_space=pl.ANY)] * 2 + [pl.BlockSpec(memory_space=pltpu.VMEM)],
        scratch_shapes=[
            pltpu.VMEM((ROWS, COLS), BF16),
            pltpu.VMEM((8, 2, ROWS, COLS), BF16),
            pltpu.VMEM((8, PIECES, ROWS, WIDTH), BF16),
            pltpu.VMEM((640, 2 * COLS), BF16),
            pltpu.VMEM((640, 2 * COLS), BF16),
            pltpu.VMEM((1, STAT), F32),
            pltpu.VMEM((len(NEAR), 1, STAT), F32),
            pltpu.VMEM((2, 1, STAT), F32),
            pltpu.VMEM((2, 1, STAT), F32),
            pltpu.VMEM((8, 2, 1, STAT), F32),
            pltpu.VMEM((1, 2 * COLS), F32),
            pltpu.VMEM((8, ROWS, SPLIT), BF16),
            pltpu.VMEM((8, ROWS, 640 - SPLIT), BF16),
            dma, dma,
            dma((16,)), dma((8, 2)),
            dma((3, SUB)), dma((8, PIECES)), dma((8, PIECES)),
            dma((len(NEAR),)), dma((len(NEAR),)), dma((2,)), dma((2,)),
            dma((8, 2)), dma((8, 2)),
            dma((2, 8)), dma((2, 8)),
        ],
        compiler_params=pltpu.CompilerParams(collective_id=0, has_side_effects=True, vmem_limit_bytes=24 << 20),
    )(derivatives, epsilon.reshape(1, ROWS))
    gram, upd = pl.pallas_call(
        assemble,
        name="assemble",
        out_shape=(jax.ShapeDtypeStruct((ROWS, 2560), F32), jax.ShapeDtypeStruct((1, COLS), F32)),
        in_specs=[pl.BlockSpec(memory_space=pltpu.VMEM)] * 3,
        out_specs=[pl.BlockSpec(memory_space=pltpu.VMEM)] * 2,
        compiler_params=pltpu.CompilerParams(vmem_limit_bytes=ASSEMBLE_VMEM),
    )(parts0, parts1, upd)
    return gram, upd.reshape(COLS)


def solution(mesh):
    in_specs = (P("smp", "par"), P("smp"))
    out_specs = (P("smp", "par"), P("par"))
    return jax.shard_map(shards, mesh=mesh, in_specs=in_specs, out_specs=out_specs, check_vma=False)
```

```python
import functools
import math

import jax
import jax.numpy as jnp
from jax import lax
from jax.experimental import pallas as pl
from jax.experimental.pallas import tpu as pltpu
from jax.sharding import PartitionSpec as P

MESH = pl.DeviceIdType.MESH
F32, BF16 = jnp.float32, jnp.bfloat16
ROWS, COLS = 80, 512
NZ, NY = 16, 4
SUB = 4
WIDTH = COLS // SUB
PIECES = 2 * SUB
SPLIT = 256
STAT = 2 * COLS + 128
NEAR = (1, -1, 2, -2, 3, -3)
FAR = 6
LOOP_FROM = 5
ASSEMBLE_VMEM = 16 << 20


def device(xh, xl, y, z, c):
    return (xl * 64 + z * NY + y, xh * 2 + c)


def kernel(total, d_ref, eps_ref, p_in0, p_in1, upd_ref,
           q_raw, r_raw, q_c, r_c, stat, z_near, z_out, z_far, p_stat, mean, p_out0, p_out1,
           q_own, q_send, q_recv, r_src, r_send, r_recv, zn_send, zn_recv, zf_send, zf_recv,
           ps_send, ps_recv, o_send, o_recv):
    s_at, p_at = lax.axis_index("smp"), lax.axis_index("par")
    xl, z, y = s_at // 64, (s_at // NY) % NZ, s_at % NY
    xh, c = p_at // 2, p_at % 2
    other = 1 - c
    half, z_lo = z // 8, z % 8
    me = xl * NY + y
    factor = 1.0 / math.sqrt(total)

    def at_z(step):
        return (z + step + NZ) % NZ

    barrier = pltpu.get_barrier_semaphore()

    def greet(where):
        pl.semaphore_signal(barrier, inc=1, device_id=where, device_id_type=MESH)

    same = (xl == xh)
    for k in range(8):
        src_xh, src_y = k // NY, k % NY

        @pl.when(jnp.logical_not(same & (src_xh == xh) & (src_y == y)))
        def _():
            greet(device(src_xh, xh, src_y, z, c))

    for k in NEAR:
        greet(device(xh, xl, y, at_z(k), c))
    for k in (1, -1):
        greet(device(xh, xl, y, at_z(k), other))
    for k in range(1, 8):
        g = (me + k) % 8
        for cc in range(2):
            greet(device(xh, g // NY, g % NY, z, cc))
    greet(device(xh, xl, y, z, other))

    pl.semaphore_wait(barrier, 8 - same.astype(jnp.int32) + len(NEAR) + 2 + 14 + 1)

    started = []

    def send(src, dst, s_sem, r_sem, where):
        copy = pltpu.make_async_remote_copy(src_ref=src, dst_ref=dst, send_sem=s_sem, recv_sem=r_sem,
                                            device_id=where, device_id_type=MESH)
        copy.start()
        return copy

    def handle(ref, sem):
        return pltpu.make_async_remote_copy(src_ref=ref, dst_ref=ref, send_sem=sem, recv_sem=sem,
                                            device_id=(s_at, p_at), device_id_type=MESH)

    def arrived(ref, sem):
        handle(ref, sem).wait_recv()

    for i in range(SUB):
        for n, q in enumerate((1, -1)):
            started.append(send(d_ref.at[:, pl.ds(i * WIDTH, WIDTH)], r_raw.at[z_lo, c * SUB + i],
                                r_src.at[n, i], r_recv.at[z_lo, c * SUB + i],
                                device(xh, xl, y, at_z(q), half)))

    d = d_ref[...].astype(F32)
    eps = eps_ref[...]
    stat[:, 0:COLS] = jnp.sum(d, axis=0, keepdims=True)
    stat[:, COLS:2 * COLS] = lax.dot_general(
        eps, d, (((1,), (0,)), ((), ())), precision=lax.Precision.HIGHEST, preferred_element_type=F32)
    stat[:, 2 * COLS:] = jnp.broadcast_to(jnp.sum(eps, axis=1, keepdims=True), (1, 128))

    for n, k in enumerate(NEAR):
        started.append(send(stat, z_near.at[n], zn_send.at[n], zn_recv.at[n], device(xh, xl, y, at_z(-k), c)))

    def own_copy(i):
        return pltpu.make_async_copy(d_ref.at[:, pl.ds(i * WIDTH, WIDTH)], r_raw.at[z_lo, c * SUB + i],
                                     r_recv.at[z_lo, c * SUB + i])

    def own_send(i):
        return pltpu.make_async_remote_copy(
            src_ref=d_ref.at[:, pl.ds(i * WIDTH, WIDTH)], dst_ref=r_raw.at[z_lo, c * SUB + i],
            send_sem=r_src.at[2, i], recv_sem=r_recv.at[z_lo, c * SUB + i],
            device_id=device(xh, xl, y, z, other), device_id_type=MESH)

    for i in range(SUB):
        @pl.when(half == c)
        def _():
            own_copy(i).start()

        @pl.when(half != c)
        def _():
            own_send(i).start()

    own_here = pltpu.make_async_copy(d_ref, q_raw.at[me, c], q_own)
    own_here.start()

    for k in range(1, 8):
        g = (me + k) % 8
        started.append(send(d_ref, q_raw.at[me, c], q_send.at[k], q_recv.at[me, c],
                            device(xh, g // NY, g % NY, z, c)))
    started.append(send(d_ref, q_raw.at[me, c], q_send.at[0], q_recv.at[me, c], device(xh, xl, y, z, other)))

    def pass_both(s):
        ways = [(sign, most, at_z(-sign * s)) for sign, most in ((1, 8), (-1, 7))]
        for j in range(PIECES):
            for sign, most, origin in ways:
                lo = origin % 8

                @pl.when((origin // 8 == c) & (s <= most))
                def _():
                    arrived(r_raw.at[lo, j], r_recv.at[lo, j])

                    @pl.when(s < most)
                    def _():
                        send(r_raw.at[lo, j], r_raw.at[lo, j], r_send.at[lo, j], r_recv.at[lo, j],
                             device(xh, xl, y, at_z(sign), c))

    pass_both(1)

    for n in range(len(NEAR)):
        arrived(z_near.at[n], zn_recv.at[n])
    up = {k: n for n, k in enumerate(NEAR)}

    def gathered(ks):
        whole = stat[...]
        for k in ks:
            whole = whole + z_near[up[k]]
        return whole

    z_out[0] = gathered((-1, 1, 2))
    z_out[1] = gathered((-2, -1, 1, 2))
    for n, k in enumerate((FAR, -FAR)):
        started.append(send(z_out.at[n], z_far.at[n], zf_send.at[n], zf_recv.at[n], device(xh, xl, y, at_z(k), c)))

    pass_both(2)
    pass_both(3)
    for n in range(2):
        arrived(z_far.at[n], zf_recv.at[n])
    p_stat[me, c] = gathered(NEAR) + z_far[0] + z_far[1]

    for k in range(1, 8):
        g = (me + k) % 8
        for cc in range(2):
            started.append(send(p_stat.at[me, c], p_stat.at[me, c], ps_send.at[k, cc], ps_recv.at[me, c],
                                device(xh, g // NY, g % NY, z, (c + cc) % 2)))
    started.append(send(p_stat.at[me, c], p_stat.at[me, c], ps_send.at[0, 0], ps_recv.at[me, c],
                        device(xh, xl, y, z, other)))
    pass_both(4)
    for k in range(1, 8):
        g = (me + k) % 8
        arrived(q_raw.at[g, c], q_recv.at[g, c])
        started.append(send(q_raw.at[g, c], q_raw.at[g, c], q_send.at[8 + k], q_recv.at[g, c],
                            device(xh, xl, y, z, other)))
    pass_both(5)
    for k in range(8):
        g = (me + k) % 8
        for cc in range(2):
            o = (c + cc) % 2
            if k or cc:
                arrived(p_stat.at[g, o], ps_recv.at[g, o])
    wholes = []
    for o in range(2):
        whole = p_stat[0, o]
        for g in range(1, 8):
            whole = whole + p_stat[g, o]
        wholes.append(whole)
        mean[:, o * COLS:(o + 1) * COLS] = whole[:, 0:COLS] / total
    mine = jnp.where(c == 0, wholes[0], wholes[1])
    upd_ref[...] = (mine[:, COLS:2 * COLS] - (mine[:, 0:COLS] / total) * mine[:, 2 * COLS:2 * COLS + 1]) * factor

    def center(raw, columns):
        return ((raw.astype(F32) - mean[:, columns]) * factor).astype(BF16)

    for k in range(8):
        g = (me + k) % 8
        if k:
            arrived(q_raw.at[g, other], q_recv.at[g, other])
        else:
            own_here.wait()
            arrived(q_raw.at[me, other], q_recv.at[me, other])

    def center_pair(u):
        for v in range(2):
            for o in range(2):
                q_c[pl.ds(u * 160 + v * ROWS, ROWS), o * COLS:(o + 1) * COLS] = center(
                    q_raw[2 * u + v, o], slice(o * COLS, (o + 1) * COLS))

    @pl.when(half == c)
    def _():
        for j in range(PIECES):
            arrived(r_raw.at[z_lo, j], r_recv.at[z_lo, j])

    slot = xh * NY + y
    outs = ((p_out0, p_in0, slice(0, SPLIT), range(4)), (p_out1, p_in1, slice(SPLIT, 640), range(3, 8)))

    def out_is_me(g):
        return same & (g == me)

    def ready_at(los):
        most = LOOP_FROM
        for v in los:
            up_steps = (z - (c * 8 + v) + NZ) % NZ
            most = jnp.maximum(most, jnp.minimum(up_steps, NZ - up_steps))
        return most

    ready = [ready_at(outs[t][3]) for t in range(2)]
    early = jnp.minimum(ready[0], ready[1]) == LOOP_FROM
    leads = (ready[0] <= ready[1], ready[1] < ready[0])
    turn = y + 2 * xh

    @pl.when(jnp.logical_not(early))
    def _():
        for u in range(4):
            center_pair(u)

    def product(t, part_at):
        p_out, p_in, columns, los = outs[t]
        for v in los if part_at == 0 else ():
            for j in range(PIECES):
                r_c[v * ROWS:(v + 1) * ROWS, j * WIDTH:(j + 1) * WIDTH] = center(
                    r_raw[v, j], slice(j * WIDTH, (j + 1) * WIDTH))
        for i in range(2 * part_at, 2 * part_at + 2):
            u = (turn + i) % 4

            @pl.when(early & leads[t])
            def _():
                center_pair(u)

            part = lax.dot_general(q_c[pl.ds(u * 160, 160), :], r_c[columns, :], (((1,), (1,)), ((), ())),
                                   preferred_element_type=F32).astype(BF16)
            for v in range(2):
                g = 2 * u + v
                p_out[g] = part[v * ROWS:(v + 1) * ROWS]

                @pl.when(out_is_me(g))
                def _():
                    pltpu.make_async_copy(p_out.at[g], p_in.at[slot], o_recv.at[t, slot]).start()

                @pl.when(jnp.logical_not(out_is_me(g)))
                def _():
                    send(p_out.at[g], p_in.at[slot], o_send.at[t, g], o_recv.at[t, slot],
                         device(xl, g // NY, g % NY, z, c))

    def step(s, carry):
        @pl.when(s > LOOP_FROM)
        def _():
            pass_both(s)

        for t in range(2):
            for part_at in range(2):
                @pl.when(jnp.minimum(ready[t] + part_at, 8) == s)
                def _():
                    product(t, part_at)
        return carry

    lax.fori_loop(LOOP_FROM, 9, step, 0)

    for copy in started:
        copy.wait_send()
    for i in range(SUB):
        @pl.when(half != c)
        def _():
            own_send(i).wait_send()
    for sign, most in ((1, 8), (-1, 7)):
        for s in range(1, most):
            origin = at_z(-sign * s)

            @pl.when(origin // 8 == c)
            def _():
                for j in range(PIECES):
                    handle(r_raw.at[origin % 8, j], r_send.at[origin % 8, j]).wait_send()
    for t in range(2):
        for g in range(8):
            @pl.when(jnp.logical_not(out_is_me(g)))
            def _():
                handle(outs[t][0].at[g], o_send.at[t, g]).wait_send()

    for t in range(2):
        for k in range(8):
            arrived(outs[t][1].at[k], o_recv.at[t, k])


def assemble(p_in0, p_in1, upd_in, gram_ref, upd_ref):
    upd_ref[...] = upd_in[...]
    for u in range(5):
        rows = slice(u * 16, (u + 1) * 16)
        added = [jnp.concatenate([p_in[k, rows].astype(F32) + p_in[NY + k, rows].astype(F32)
                                  for p_in in (p_in0, p_in1)], axis=1) for k in range(NY)]
        for w in range(4):
            gram_ref[rows, w * 640:(w + 1) * 640] = jnp.concatenate(
                [added[k][:, (2 * w + v) * ROWS:(2 * w + v + 1) * ROWS] for v in range(2) for k in range(NY)], axis=1)


def shards(derivatives, epsilon):
    total = derivatives.shape[0] * 128
    dma = pltpu.SemaphoreType.DMA
    parts0, parts1, upd = pl.pallas_call(
        functools.partial(kernel, total),
        name="gram",
        out_shape=(jax.ShapeDtypeStruct((8, ROWS, SPLIT), BF16), jax.ShapeDtypeStruct((8, ROWS, 640 - SPLIT), BF16),
                   jax.ShapeDtypeStruct((1, COLS), F32)),
        in_specs=[pl.BlockSpec(memory_space=pltpu.VMEM)] * 2,
        out_specs=[pl.BlockSpec(memory_space=pl.ANY)] * 2 + [pl.BlockSpec(memory_space=pltpu.VMEM)],
        scratch_shapes=[
            pltpu.VMEM((8, 2, ROWS, COLS), BF16),
            pltpu.VMEM((8, PIECES, ROWS, WIDTH), BF16),
            pltpu.VMEM((640, 2 * COLS), BF16),
            pltpu.VMEM((640, 2 * COLS), BF16),
            pltpu.VMEM((1, STAT), F32),
            pltpu.VMEM((len(NEAR), 1, STAT), F32),
            pltpu.VMEM((2, 1, STAT), F32),
            pltpu.VMEM((2, 1, STAT), F32),
            pltpu.VMEM((8, 2, 1, STAT), F32),
            pltpu.VMEM((1, 2 * COLS), F32),
            pltpu.VMEM((8, ROWS, SPLIT), BF16),
            pltpu.VMEM((8, ROWS, 640 - SPLIT), BF16),
            dma,
            dma((16,)), dma((8, 2)),
            dma((3, SUB)), dma((8, PIECES)), dma((8, PIECES)),
            dma((len(NEAR),)), dma((len(NEAR),)), dma((2,)), dma((2,)),
            dma((8, 2)), dma((8, 2)),
            dma((2, 8)), dma((2, 8)),
        ],
        compiler_params=pltpu.CompilerParams(collective_id=0, has_side_effects=True, vmem_limit_bytes=24 << 20),
    )(derivatives, epsilon.reshape(1, ROWS))
    gram, upd = pl.pallas_call(
        assemble,
        name="assemble",
        out_shape=(jax.ShapeDtypeStruct((ROWS, 2560), F32), jax.ShapeDtypeStruct((1, COLS), F32)),
        in_specs=[pl.BlockSpec(memory_space=pltpu.VMEM)] * 3,
        out_specs=[pl.BlockSpec(memory_space=pltpu.VMEM)] * 2,
        compiler_params=pltpu.CompilerParams(vmem_limit_bytes=ASSEMBLE_VMEM),
    )(parts0, parts1, upd)
    return gram, upd.reshape(COLS)


def solution(mesh):
    in_specs = (P("smp", "par"), P("smp"))
    out_specs = (P("smp", "par"), P("par"))
    return jax.shard_map(shards, mesh=mesh, in_specs=in_specs, out_specs=out_specs, check_vma=False)
```

```python
import functools
import math

import jax
import jax.numpy as jnp
from jax import lax
from jax.experimental import pallas as pl
from jax.experimental.pallas import tpu as pltpu
from jax.sharding import PartitionSpec as P

MESH = pl.DeviceIdType.MESH
F32, BF16 = jnp.float32, jnp.bfloat16
ROWS, COLS = 80, 512
NZ, NY = 16, 4
SUB = 4
WIDTH = COLS // SUB
PIECES = 2 * SUB
SPLIT = 256
STAT = 2 * COLS + 128
NEAR = (1, -1, 2, -2, 3, -3)
FAR = 6
LOOP_FROM = 5
ASSEMBLE_VMEM = 16 << 20


def device(xh, xl, y, z, c):
    return (xl * 64 + z * NY + y, xh * 2 + c)


def kernel(total, d_ref, eps_ref, p_in0, p_in1, upd_ref,
           q_raw, r_raw, q_c, r_c, stat, z_near, z_out, z_far, p_stat, mean, p_out0, p_out1,
           q_own, q_send, q_recv, r_src, r_send, r_recv, zn_send, zn_recv, zf_send, zf_recv,
           ps_send, ps_recv, o_send, o_recv):
    s_at, p_at = lax.axis_index("smp"), lax.axis_index("par")
    xl, z, y = s_at // 64, (s_at // NY) % NZ, s_at % NY
    xh, c = p_at // 2, p_at % 2
    other = 1 - c
    half, z_lo = z // 8, z % 8
    me = xl * NY + y
    factor = 1.0 / math.sqrt(total)

    def at_z(step):
        return (z + step + NZ) % NZ

    barrier = pltpu.get_barrier_semaphore()

    def greet(where):
        pl.semaphore_signal(barrier, inc=1, device_id=where, device_id_type=MESH)

    same = (xl == xh)
    for k in range(8):
        src_xh, src_y = k // NY, k % NY

        @pl.when(jnp.logical_not(same & (src_xh == xh) & (src_y == y)))
        def _():
            greet(device(src_xh, xh, src_y, z, c))

    for k in NEAR:
        greet(device(xh, xl, y, at_z(k), c))
    for k in (1, -1):
        greet(device(xh, xl, y, at_z(k), other))
    for k in range(1, 8):
        g = (me + k) % 8
        for cc in range(2):
            greet(device(xh, g // NY, g % NY, z, cc))
    greet(device(xh, xl, y, z, other))

    pl.semaphore_wait(barrier, 8 - same.astype(jnp.int32) + len(NEAR) + 2 + 14 + 1)

    started = []

    def send(src, dst, s_sem, r_sem, where):
        copy = pltpu.make_async_remote_copy(src_ref=src, dst_ref=dst, send_sem=s_sem, recv_sem=r_sem,
                                            device_id=where, device_id_type=MESH)
        copy.start()
        return copy

    def handle(ref, sem):
        return pltpu.make_async_remote_copy(src_ref=ref, dst_ref=ref, send_sem=sem, recv_sem=sem,
                                            device_id=(s_at, p_at), device_id_type=MESH)

    def arrived(ref, sem):
        handle(ref, sem).wait_recv()

    for i in range(SUB):
        for n, q in enumerate((1, -1)):
            started.append(send(d_ref.at[:, pl.ds(i * WIDTH, WIDTH)], r_raw.at[z_lo, c * SUB + i],
                                r_src.at[n, i], r_recv.at[z_lo, c * SUB + i],
                                device(xh, xl, y, at_z(q), half)))

    d = d_ref[...].astype(F32)
    eps = eps_ref[...]
    stat[:, 0:COLS] = jnp.sum(d, axis=0, keepdims=True)
    stat[:, COLS:2 * COLS] = lax.dot_general(
        eps, d, (((1,), (0,)), ((), ())), precision=lax.Precision.HIGHEST, preferred_element_type=F32)
    stat[:, 2 * COLS:] = jnp.broadcast_to(jnp.sum(eps, axis=1, keepdims=True), (1, 128))

    for n, k in enumerate(NEAR):
        started.append(send(stat, z_near.at[n], zn_send.at[n], zn_recv.at[n], device(xh, xl, y, at_z(-k), c)))

    def own_copy(i):
        return pltpu.make_async_copy(d_ref.at[:, pl.ds(i * WIDTH, WIDTH)], r_raw.at[z_lo, c * SUB + i],
                                     r_recv.at[z_lo, c * SUB + i])

    def own_send(i):
        return pltpu.make_async_remote_copy(
            src_ref=d_ref.at[:, pl.ds(i * WIDTH, WIDTH)], dst_ref=r_raw.at[z_lo, c * SUB + i],
            send_sem=r_src.at[2, i], recv_sem=r_recv.at[z_lo, c * SUB + i],
            device_id=device(xh, xl, y, z, other), device_id_type=MESH)

    for i in range(SUB):
        @pl.when(half == c)
        def _():
            own_copy(i).start()

        @pl.when(half != c)
        def _():
            own_send(i).start()

    own_here = pltpu.make_async_copy(d_ref, q_raw.at[me, c], q_own)
    own_here.start()

    for k in range(1, 8):
        g = (me + k) % 8
        started.append(send(d_ref, q_raw.at[me, c], q_send.at[k], q_recv.at[me, c],
                            device(xh, g // NY, g % NY, z, c)))
    started.append(send(d_ref, q_raw.at[me, c], q_send.at[0], q_recv.at[me, c], device(xh, xl, y, z, other)))

    def pass_both(s):
        ways = [(sign, most, at_z(-sign * s)) for sign, most in ((1, 8), (-1, 7))]
        for j in range(PIECES):
            for sign, most, origin in ways:
                lo = origin % 8

                @pl.when((origin // 8 == c) & (s <= most))
                def _():
                    arrived(r_raw.at[lo, j], r_recv.at[lo, j])

                    @pl.when(s < most)
                    def _():
                        send(r_raw.at[lo, j], r_raw.at[lo, j], r_send.at[lo, j], r_recv.at[lo, j],
                             device(xh, xl, y, at_z(sign), c))

    pass_both(1)

    for n in range(len(NEAR)):
        arrived(z_near.at[n], zn_recv.at[n])
    up = {k: n for n, k in enumerate(NEAR)}

    def gathered(ks):
        whole = stat[...]
        for k in ks:
            whole = whole + z_near[up[k]]
        return whole

    z_out[0] = gathered((-1, 1, 2))
    z_out[1] = gathered((-2, -1, 1, 2))
    for n, k in enumerate((FAR, -FAR)):
        started.append(send(z_out.at[n], z_far.at[n], zf_send.at[n], zf_recv.at[n], device(xh, xl, y, at_z(k), c)))

    pass_both(2)
    pass_both(3)
    for n in range(2):
        arrived(z_far.at[n], zf_recv.at[n])
    p_stat[me, c] = gathered(NEAR) + z_far[0] + z_far[1]

    for k in range(1, 8):
        g = (me + k) % 8
        for cc in range(2):
            started.append(send(p_stat.at[me, c], p_stat.at[me, c], ps_send.at[k, cc], ps_recv.at[me, c],
                                device(xh, g // NY, g % NY, z, (c + cc) % 2)))
    started.append(send(p_stat.at[me, c], p_stat.at[me, c], ps_send.at[0, 0], ps_recv.at[me, c],
                        device(xh, xl, y, z, other)))
    pass_both(4)
    for k in range(1, 8):
        g = (me + k) % 8
        arrived(q_raw.at[g, c], q_recv.at[g, c])
        started.append(send(q_raw.at[g, c], q_raw.at[g, c], q_send.at[8 + k], q_recv.at[g, c],
                            device(xh, xl, y, z, other)))
    pass_both(5)
    for k in range(8):
        g = (me + k) % 8
        for cc in range(2):
            o = (c + cc) % 2
            if k or cc:
                arrived(p_stat.at[g, o], ps_recv.at[g, o])
    wholes = []
    for o in range(2):
        whole = p_stat[0, o]
        for g in range(1, 8):
            whole = whole + p_stat[g, o]
        wholes.append(whole)
        mean[:, o * COLS:(o + 1) * COLS] = whole[:, 0:COLS] / total
    mine = jnp.where(c == 0, wholes[0], wholes[1])
    upd_ref[...] = (mine[:, COLS:2 * COLS] - (mine[:, 0:COLS] / total) * mine[:, 2 * COLS:2 * COLS + 1]) * factor

    def center(raw, columns):
        return ((raw.astype(F32) - mean[:, columns]) * factor).astype(BF16)

    for k in range(8):
        g = (me + k) % 8
        if k:
            arrived(q_raw.at[g, other], q_recv.at[g, other])
        else:
            own_here.wait()
            arrived(q_raw.at[me, other], q_recv.at[me, other])

    def center_pair(u):
        for v in range(2):
            for o in range(2):
                q_c[pl.ds(u * 160 + v * ROWS, ROWS), o * COLS:(o + 1) * COLS] = center(
                    q_raw[2 * u + v, o], slice(o * COLS, (o + 1) * COLS))

    @pl.when(half == c)
    def _():
        for j in range(PIECES):
            arrived(r_raw.at[z_lo, j], r_recv.at[z_lo, j])

    slot = xh * NY + y
    outs = ((p_out0, p_in0, slice(0, SPLIT), range(4)), (p_out1, p_in1, slice(SPLIT, 640), range(3, 8)))

    def out_is_me(g):
        return same & (g == me)

    def ready_at(los):
        most = LOOP_FROM
        for v in los:
            up_steps = (z - (c * 8 + v) + NZ) % NZ
            most = jnp.maximum(most, jnp.minimum(up_steps, NZ - up_steps))
        return most

    ready = [ready_at(outs[t][3]) for t in range(2)]
    early = jnp.minimum(ready[0], ready[1]) == LOOP_FROM
    leads = (ready[0] <= ready[1], ready[1] < ready[0])
    turn = y + 2 * xh

    def product(t, part_at):
        p_out, p_in, columns, los = outs[t]
        for v in los if part_at == 0 else ():
            for j in range(PIECES):
                r_c[v * ROWS:(v + 1) * ROWS, j * WIDTH:(j + 1) * WIDTH] = center(
                    r_raw[v, j], slice(j * WIDTH, (j + 1) * WIDTH))
        for i in range(2 * part_at, 2 * part_at + 2):
            u = (turn + i) % 4

            @pl.when(early & leads[t])
            def _():
                center_pair(u)

            part = lax.dot_general(q_c[pl.ds(u * 160, 160), :], r_c[columns, :], (((1,), (1,)), ((), ())),
                                   preferred_element_type=F32).astype(BF16)
            for v in range(2):
                g = 2 * u + v
                p_out[g] = part[v * ROWS:(v + 1) * ROWS]

                @pl.when(out_is_me(g))
                def _():
                    pltpu.make_async_copy(p_out.at[g], p_in.at[slot], o_recv.at[t, slot]).start()

                @pl.when(jnp.logical_not(out_is_me(g)))
                def _():
                    send(p_out.at[g], p_in.at[slot], o_send.at[t, g], o_recv.at[t, slot],
                         device(xl, g // NY, g % NY, z, c))

    def step(s, carry):
        @pl.when(s > LOOP_FROM)
        def _():
            pass_both(s)

        @pl.when(jnp.logical_not(early) & (s == LOOP_FROM + 1))
        def _():
            for u in range(4):
                center_pair(u)

        for t in range(2):
            for part_at in range(2):
                @pl.when(jnp.minimum(ready[t] + part_at, 8) == s)
                def _():
                    product(t, part_at)
        return carry

    lax.fori_loop(LOOP_FROM, 9, step, 0)

    for copy in started:
        copy.wait_send()
    for i in range(SUB):
        @pl.when(half != c)
        def _():
            own_send(i).wait_send()
    for sign, most in ((1, 8), (-1, 7)):
        for s in range(1, most):
            origin = at_z(-sign * s)

            @pl.when(origin // 8 == c)
            def _():
                for j in range(PIECES):
                    handle(r_raw.at[origin % 8, j], r_send.at[origin % 8, j]).wait_send()
    for t in range(2):
        for g in range(8):
            @pl.when(jnp.logical_not(out_is_me(g)))
            def _():
                handle(outs[t][0].at[g], o_send.at[t, g]).wait_send()

    for t in range(2):
        for k in range(8):
            arrived(outs[t][1].at[k], o_recv.at[t, k])


def assemble(p_in0, p_in1, upd_in, gram_ref, upd_ref):
    upd_ref[...] = upd_in[...]
    for u in range(5):
        rows = slice(u * 16, (u + 1) * 16)
        added = [jnp.concatenate([p_in[k, rows].astype(F32) + p_in[NY + k, rows].astype(F32)
                                  for p_in in (p_in0, p_in1)], axis=1) for k in range(NY)]
        for w in range(4):
            gram_ref[rows, w * 640:(w + 1) * 640] = jnp.concatenate(
                [added[k][:, (2 * w + v) * ROWS:(2 * w + v + 1) * ROWS] for v in range(2) for k in range(NY)], axis=1)


def shards(derivatives, epsilon):
    total = derivatives.shape[0] * 128
    dma = pltpu.SemaphoreType.DMA
    parts0, parts1, upd = pl.pallas_call(
        functools.partial(kernel, total),
        name="gram",
        out_shape=(jax.ShapeDtypeStruct((8, ROWS, SPLIT), BF16), jax.ShapeDtypeStruct((8, ROWS, 640 - SPLIT), BF16),
                   jax.ShapeDtypeStruct((1, COLS), F32)),
        in_specs=[pl.BlockSpec(memory_space=pltpu.VMEM)] * 2,
        out_specs=[pl.BlockSpec(memory_space=pl.ANY)] * 2 + [pl.BlockSpec(memory_space=pltpu.VMEM)],
        scratch_shapes=[
            pltpu.VMEM((8, 2, ROWS, COLS), BF16),
            pltpu.VMEM((8, PIECES, ROWS, WIDTH), BF16),
            pltpu.VMEM((640, 2 * COLS), BF16),
            pltpu.VMEM((640, 2 * COLS), BF16),
            pltpu.VMEM((1, STAT), F32),
            pltpu.VMEM((len(NEAR), 1, STAT), F32),
            pltpu.VMEM((2, 1, STAT), F32),
            pltpu.VMEM((2, 1, STAT), F32),
            pltpu.VMEM((8, 2, 1, STAT), F32),
            pltpu.VMEM((1, 2 * COLS), F32),
            pltpu.VMEM((8, ROWS, SPLIT), BF16),
            pltpu.VMEM((8, ROWS, 640 - SPLIT), BF16),
            dma,
            dma((16,)), dma((8, 2)),
            dma((3, SUB)), dma((8, PIECES)), dma((8, PIECES)),
            dma((len(NEAR),)), dma((len(NEAR),)), dma((2,)), dma((2,)),
            dma((8, 2)), dma((8, 2)),
            dma((2, 8)), dma((2, 8)),
        ],
        compiler_params=pltpu.CompilerParams(collective_id=0, has_side_effects=True, vmem_limit_bytes=24 << 20),
    )(derivatives, epsilon.reshape(1, ROWS))
    gram, upd = pl.pallas_call(
        assemble,
        name="assemble",
        out_shape=(jax.ShapeDtypeStruct((ROWS, 2560), F32), jax.ShapeDtypeStruct((1, COLS), F32)),
        in_specs=[pl.BlockSpec(memory_space=pltpu.VMEM)] * 3,
        out_specs=[pl.BlockSpec(memory_space=pltpu.VMEM)] * 2,
        compiler_params=pltpu.CompilerParams(vmem_limit_bytes=ASSEMBLE_VMEM),
    )(parts0, parts1, upd)
    return gram, upd.reshape(COLS)


def solution(mesh):
    in_specs = (P("smp", "par"), P("smp"))
    out_specs = (P("smp", "par"), P("par"))
    return jax.shard_map(shards, mesh=mesh, in_specs=in_specs, out_specs=out_specs, check_vma=False)
```

```python
import functools
import math

import jax
import jax.numpy as jnp
from jax import lax
from jax.experimental import pallas as pl
from jax.experimental.pallas import tpu as pltpu
from jax.sharding import PartitionSpec as P

MESH = pl.DeviceIdType.MESH
F32, BF16 = jnp.float32, jnp.bfloat16
ROWS, COLS = 80, 512
NZ, NY = 16, 4
SUB = 4
WIDTH = COLS // SUB
PIECES = 2 * SUB
SPLIT = 384
STAT = 2 * COLS + 128
NEAR = (1, -1, 2, -2, 3, -3)
FAR = 6
LOOP_FROM = 5
ASSEMBLE_VMEM = 16 << 20


def device(xh, xl, y, z, c):
    return (xl * 64 + z * NY + y, xh * 2 + c)


def kernel(total, d_ref, eps_ref, p_in0, p_in1, upd_ref,
           q_raw, r_raw, q_c, r_c, stat, z_near, z_out, z_far, p_stat, mean, p_out0, p_out1,
           q_own, q_send, q_recv, r_src, r_send, r_recv, zn_send, zn_recv, zf_send, zf_recv,
           ps_send, ps_recv, o_send, o_recv):
    s_at, p_at = lax.axis_index("smp"), lax.axis_index("par")
    xl, z, y = s_at // 64, (s_at // NY) % NZ, s_at % NY
    xh, c = p_at // 2, p_at % 2
    other = 1 - c
    half, z_lo = z // 8, z % 8
    me = xl * NY + y
    factor = 1.0 / math.sqrt(total)

    def at_z(step):
        return (z + step + NZ) % NZ

    barrier = pltpu.get_barrier_semaphore()

    def greet(where):
        pl.semaphore_signal(barrier, inc=1, device_id=where, device_id_type=MESH)

    same = (xl == xh)
    for k in range(8):
        src_xh, src_y = k // NY, k % NY

        @pl.when(jnp.logical_not(same & (src_xh == xh) & (src_y == y)))
        def _():
            greet(device(src_xh, xh, src_y, z, c))

    for k in NEAR:
        greet(device(xh, xl, y, at_z(k), c))
    for k in (1, -1):
        greet(device(xh, xl, y, at_z(k), other))
    for k in range(1, 8):
        g = (me + k) % 8
        for cc in range(2):
            greet(device(xh, g // NY, g % NY, z, cc))
    greet(device(xh, xl, y, z, other))

    pl.semaphore_wait(barrier, 8 - same.astype(jnp.int32) + len(NEAR) + 2 + 14 + 1)

    started = []

    def send(src, dst, s_sem, r_sem, where):
        copy = pltpu.make_async_remote_copy(src_ref=src, dst_ref=dst, send_sem=s_sem, recv_sem=r_sem,
                                            device_id=where, device_id_type=MESH)
        copy.start()
        return copy

    def handle(ref, sem):
        return pltpu.make_async_remote_copy(src_ref=ref, dst_ref=ref, send_sem=sem, recv_sem=sem,
                                            device_id=(s_at, p_at), device_id_type=MESH)

    def arrived(ref, sem):
        handle(ref, sem).wait_recv()

    for i in range(SUB):
        for n, q in enumerate((1, -1)):
            started.append(send(d_ref.at[:, pl.ds(i * WIDTH, WIDTH)], r_raw.at[z_lo, c * SUB + i],
                                r_src.at[n, i], r_recv.at[z_lo, c * SUB + i],
                                device(xh, xl, y, at_z(q), half)))

    d = d_ref[...].astype(F32)
    eps = eps_ref[...]
    stat[:, 0:COLS] = jnp.sum(d, axis=0, keepdims=True)
    stat[:, COLS:2 * COLS] = lax.dot_general(
        eps, d, (((1,), (0,)), ((), ())), precision=lax.Precision.HIGHEST, preferred_element_type=F32)
    stat[:, 2 * COLS:] = jnp.broadcast_to(jnp.sum(eps, axis=1, keepdims=True), (1, 128))

    for n, k in enumerate(NEAR):
        started.append(send(stat, z_near.at[n], zn_send.at[n], zn_recv.at[n], device(xh, xl, y, at_z(-k), c)))

    def own_copy(i):
        return pltpu.make_async_copy(d_ref.at[:, pl.ds(i * WIDTH, WIDTH)], r_raw.at[z_lo, c * SUB + i],
                                     r_recv.at[z_lo, c * SUB + i])

    def own_send(i):
        return pltpu.make_async_remote_copy(
            src_ref=d_ref.at[:, pl.ds(i * WIDTH, WIDTH)], dst_ref=r_raw.at[z_lo, c * SUB + i],
            send_sem=r_src.at[2, i], recv_sem=r_recv.at[z_lo, c * SUB + i],
            device_id=device(xh, xl, y, z, other), device_id_type=MESH)

    for i in range(SUB):
        @pl.when(half == c)
        def _():
            own_copy(i).start()

        @pl.when(half != c)
        def _():
            own_send(i).start()

    own_here = pltpu.make_async_copy(d_ref, q_raw.at[me, c], q_own)
    own_here.start()

    for k in range(1, 8):
        g = (me + k) % 8
        started.append(send(d_ref, q_raw.at[me, c], q_send.at[k], q_recv.at[me, c],
                            device(xh, g // NY, g % NY, z, c)))
    started.append(send(d_ref, q_raw.at[me, c], q_send.at[0], q_recv.at[me, c], device(xh, xl, y, z, other)))

    def pass_both(s):
        ways = [(sign, most, at_z(-sign * s)) for sign, most in ((1, 8), (-1, 7))]
        for j in range(PIECES):
            for sign, most, origin in ways:
                lo = origin % 8

                @pl.when((origin // 8 == c) & (s <= most))
                def _():
                    arrived(r_raw.at[lo, j], r_recv.at[lo, j])

                    @pl.when(s < most)
                    def _():
                        send(r_raw.at[lo, j], r_raw.at[lo, j], r_send.at[lo, j], r_recv.at[lo, j],
                             device(xh, xl, y, at_z(sign), c))

    pass_both(1)

    for n in range(len(NEAR)):
        arrived(z_near.at[n], zn_recv.at[n])
    up = {k: n for n, k in enumerate(NEAR)}

    def gathered(ks):
        whole = stat[...]
        for k in ks:
            whole = whole + z_near[up[k]]
        return whole

    z_out[0] = gathered((-1, 1, 2))
    z_out[1] = gathered((-2, -1, 1, 2))
    for n, k in enumerate((FAR, -FAR)):
        started.append(send(z_out.at[n], z_far.at[n], zf_send.at[n], zf_recv.at[n], device(xh, xl, y, at_z(k), c)))

    pass_both(2)
    pass_both(3)
    for n in range(2):
        arrived(z_far.at[n], zf_recv.at[n])
    p_stat[me, c] = gathered(NEAR) + z_far[0] + z_far[1]

    for k in range(1, 8):
        g = (me + k) % 8
        for cc in range(2):
            started.append(send(p_stat.at[me, c], p_stat.at[me, c], ps_send.at[k, cc], ps_recv.at[me, c],
                                device(xh, g // NY, g % NY, z, (c + cc) % 2)))
    started.append(send(p_stat.at[me, c], p_stat.at[me, c], ps_send.at[0, 0], ps_recv.at[me, c],
                        device(xh, xl, y, z, other)))
    pass_both(4)
    for k in range(1, 8):
        g = (me + k) % 8
        arrived(q_raw.at[g, c], q_recv.at[g, c])
        started.append(send(q_raw.at[g, c], q_raw.at[g, c], q_send.at[8 + k], q_recv.at[g, c],
                            device(xh, xl, y, z, other)))
    pass_both(5)
    for k in range(8):
        g = (me + k) % 8
        for cc in range(2):
            o = (c + cc) % 2
            if k or cc:
                arrived(p_stat.at[g, o], ps_recv.at[g, o])
    wholes = []
    for o in range(2):
        whole = p_stat[0, o]
        for g in range(1, 8):
            whole = whole + p_stat[g, o]
        wholes.append(whole)
        mean[:, o * COLS:(o + 1) * COLS] = whole[:, 0:COLS] / total
    mine = jnp.where(c == 0, wholes[0], wholes[1])
    upd_ref[...] = (mine[:, COLS:2 * COLS] - (mine[:, 0:COLS] / total) * mine[:, 2 * COLS:2 * COLS + 1]) * factor

    def center(raw, columns):
        return ((raw.astype(F32) - mean[:, columns]) * factor).astype(BF16)

    for k in range(8):
        g = (me + k) % 8
        if k:
            arrived(q_raw.at[g, other], q_recv.at[g, other])
        else:
            own_here.wait()
            arrived(q_raw.at[me, other], q_recv.at[me, other])

    def center_pair(u):
        for v in range(2):
            for o in range(2):
                q_c[pl.ds(u * 160 + v * ROWS, ROWS), o * COLS:(o + 1) * COLS] = center(
                    q_raw[2 * u + v, o], slice(o * COLS, (o + 1) * COLS))

    @pl.when(half == c)
    def _():
        for j in range(PIECES):
            arrived(r_raw.at[z_lo, j], r_recv.at[z_lo, j])

    slot = xh * NY + y
    outs = ((p_out0, p_in0, slice(0, SPLIT), range(5)), (p_out1, p_in1, slice(SPLIT, 640), range(4, 8)))

    def out_is_me(g):
        return same & (g == me)

    def ready_at(los):
        most = LOOP_FROM
        for v in los:
            up_steps = (z - (c * 8 + v) + NZ) % NZ
            most = jnp.maximum(most, jnp.minimum(up_steps, NZ - up_steps))
        return most

    ready = [ready_at(outs[t][3]) for t in range(2)]
    early = jnp.minimum(ready[0], ready[1]) == LOOP_FROM
    leads = (ready[0] <= ready[1], ready[1] < ready[0])
    turn = y + 2 * xh

    @pl.when(jnp.logical_not(early))
    def _():
        for u in range(4):
            center_pair(u)

    def product(t, part_at):
        p_out, p_in, columns, los = outs[t]
        for v in los if part_at == 0 else ():
            for j in range(PIECES):
                r_c[v * ROWS:(v + 1) * ROWS, j * WIDTH:(j + 1) * WIDTH] = center(
                    r_raw[v, j], slice(j * WIDTH, (j + 1) * WIDTH))
        for i in range(2 * part_at, 2 * part_at + 2):
            u = (turn + i) % 4

            @pl.when(early & leads[t])
            def _():
                center_pair(u)

            part = lax.dot_general(q_c[pl.ds(u * 160, 160), :], r_c[columns, :], (((1,), (1,)), ((), ())),
                                   preferred_element_type=F32).astype(BF16)
            for v in range(2):
                g = 2 * u + v
                p_out[g] = part[v * ROWS:(v + 1) * ROWS]

                @pl.when(out_is_me(g))
                def _():
                    pltpu.make_async_copy(p_out.at[g], p_in.at[slot], o_recv.at[t, slot]).start()

                @pl.when(jnp.logical_not(out_is_me(g)))
                def _():
                    send(p_out.at[g], p_in.at[slot], o_send.at[t, g], o_recv.at[t, slot],
                         device(xl, g // NY, g % NY, z, c))

    def step(s, carry):
        @pl.when(s > LOOP_FROM)
        def _():
            pass_both(s)

        for t in range(2):
            for part_at in range(2):
                @pl.when(jnp.minimum(ready[t] + part_at, 8) == s)
                def _():
                    product(t, part_at)
        return carry

    lax.fori_loop(LOOP_FROM, 9, step, 0)

    for copy in started:
        copy.wait_send()
    for i in range(SUB):
        @pl.when(half != c)
        def _():
            own_send(i).wait_send()
    for sign, most in ((1, 8), (-1, 7)):
        for s in range(1, most):
            origin = at_z(-sign * s)

            @pl.when(origin // 8 == c)
            def _():
                for j in range(PIECES):
                    handle(r_raw.at[origin % 8, j], r_send.at[origin % 8, j]).wait_send()
    for t in range(2):
        for g in range(8):
            @pl.when(jnp.logical_not(out_is_me(g)))
            def _():
                handle(outs[t][0].at[g], o_send.at[t, g]).wait_send()

    for t in range(2):
        for k in range(8):
            arrived(outs[t][1].at[k], o_recv.at[t, k])


def assemble(p_in0, p_in1, upd_in, gram_ref, upd_ref):
    upd_ref[...] = upd_in[...]
    for u in range(5):
        rows = slice(u * 16, (u + 1) * 16)
        added = [jnp.concatenate([p_in[k, rows].astype(F32) + p_in[NY + k, rows].astype(F32)
                                  for p_in in (p_in0, p_in1)], axis=1) for k in range(NY)]
        for w in range(4):
            gram_ref[rows, w * 640:(w + 1) * 640] = jnp.concatenate(
                [added[k][:, (2 * w + v) * ROWS:(2 * w + v + 1) * ROWS] for v in range(2) for k in range(NY)], axis=1)


def shards(derivatives, epsilon):
    total = derivatives.shape[0] * 128
    dma = pltpu.SemaphoreType.DMA
    parts0, parts1, upd = pl.pallas_call(
        functools.partial(kernel, total),
        name="gram",
        out_shape=(jax.ShapeDtypeStruct((8, ROWS, SPLIT), BF16), jax.ShapeDtypeStruct((8, ROWS, 640 - SPLIT), BF16),
                   jax.ShapeDtypeStruct((1, COLS), F32)),
        in_specs=[pl.BlockSpec(memory_space=pltpu.VMEM)] * 2,
        out_specs=[pl.BlockSpec(memory_space=pl.ANY)] * 2 + [pl.BlockSpec(memory_space=pltpu.VMEM)],
        scratch_shapes=[
            pltpu.VMEM((8, 2, ROWS, COLS), BF16),
            pltpu.VMEM((8, PIECES, ROWS, WIDTH), BF16),
            pltpu.VMEM((640, 2 * COLS), BF16),
            pltpu.VMEM((640, 2 * COLS), BF16),
            pltpu.VMEM((1, STAT), F32),
            pltpu.VMEM((len(NEAR), 1, STAT), F32),
            pltpu.VMEM((2, 1, STAT), F32),
            pltpu.VMEM((2, 1, STAT), F32),
            pltpu.VMEM((8, 2, 1, STAT), F32),
            pltpu.VMEM((1, 2 * COLS), F32),
            pltpu.VMEM((8, ROWS, SPLIT), BF16),
            pltpu.VMEM((8, ROWS, 640 - SPLIT), BF16),
            dma,
            dma((16,)), dma((8, 2)),
            dma((3, SUB)), dma((8, PIECES)), dma((8, PIECES)),
            dma((len(NEAR),)), dma((len(NEAR),)), dma((2,)), dma((2,)),
            dma((8, 2)), dma((8, 2)),
            dma((2, 8)), dma((2, 8)),
        ],
        compiler_params=pltpu.CompilerParams(collective_id=0, has_side_effects=True, vmem_limit_bytes=24 << 20),
    )(derivatives, epsilon.reshape(1, ROWS))
    gram, upd = pl.pallas_call(
        assemble,
        name="assemble",
        out_shape=(jax.ShapeDtypeStruct((ROWS, 2560), F32), jax.ShapeDtypeStruct((1, COLS), F32)),
        in_specs=[pl.BlockSpec(memory_space=pltpu.VMEM)] * 3,
        out_specs=[pl.BlockSpec(memory_space=pltpu.VMEM)] * 2,
        compiler_params=pltpu.CompilerParams(vmem_limit_bytes=ASSEMBLE_VMEM),
    )(parts0, parts1, upd)
    return gram, upd.reshape(COLS)


def solution(mesh):
    in_specs = (P("smp", "par"), P("smp"))
    out_specs = (P("smp", "par"), P("par"))
    return jax.shard_map(shards, mesh=mesh, in_specs=in_specs, out_specs=out_specs, check_vma=False)
```
